768 devices in a mesh: dp: 96 (over z, y), expert: 8 (over x, core).
Axes of the slice: x: 4, y: 8, z: 12, core: 2. Of those that a mesh axis runs over, the one named last changes fastest.
Arguments:
- tokens: bfloat16 [98304, 1024], P(('dp', 'expert')), may hold values from -6 to 6
- cotangent: bfloat16 [98304, 1024], P(('dp', 'expert')), may hold values from -6 to 6
- expert_ids: int32 [98304, 2], P(('dp', 'expert')), may hold values from 0 to 7, all different within a row; in each aligned block of 128 rows (0 to 127, 128 to 255, ...) at most 64 rows name the same one
- route_weights: bfloat16 [98304, 2], P(('dp', 'expert')), may hold values from 0.099609375 to 1
- expert_weights: bfloat16 [8, 1536, 1024], P('expert'), may hold values from -0.1875 to 0.1875
Outputs:
- latent_out: bfloat16 [98304, 1024], P(('dp', 'expert'))
- token_grad: bfloat16 [98304, 1024], P(('dp', 'expert'))
- route_grad: float32 [98304, 2], P(('dp', 'expert'))
- expert_grads: float32 [8, 1536, 1024], P('expert', 'dp')
The draws below stay inside these ranges and needn't reach their ends.
Inputs may be any that keep to these rules, and one draw needn't show every extreme that they name: `expert_ids`: each token names 2 different experts. In each aligned block of 128 tokens (the tokens of one device) no expert is named by more than 64 tokens, and in some blocks one expert is named by exactly 64.
All inputs are finite; a program needn't handle non-finite values.
Results may differ from the reference program's by a relative error of at most 0.0065.
Values may be sent and summed in bfloat16 or wider, within the bound.
A program may use at most 32 MiB of HBM per device.

```python
import math
import jax
import jax.numpy as jnp
import numpy as np
from jax import lax

LATENT = 1024
HIDDEN_SIZE = 512
TOP_K = 2
TOK_DEV = 128
CAPACITY = 64
EXPERTS = 8
TOKENS = 98304
N_DP = 96
N_EXPERT = 8


def steps_of(key, extent, shards, low, high):
    factor_of = 1.0
    for position, parts in shards:
        draws = jax.random.uniform(jax.random.fold_in(jax.random.fold_in(key, 6), position), (parts,), jnp.float32, low / len(shards), high / len(shards))
        factor_of = factor_of * jnp.repeat(jnp.exp(draws), extent[position] // parts).reshape((-1,) + (1,) * (len(extent) - 1 - position))
    return factor_of


def shared_out(stream_key, own, number, rows, count, top, most, slope):
    ranking = jax.random.permutation(stream_key, count)
    heavy_load, usual = shares(count, rows * top, most, slope, True), shares(count, rows * top, most, slope, False)
    places = jnp.arange(count)

    def named(sizes, offset_by):
        used = int((sizes > 0).sum())
        fixed = max(1, used // 4)
        shifted = fixed + (places - fixed + offset_by * (used - fixed)) % max(1, count - fixed)
        return jnp.zeros((count,), jnp.int32).at[ranking[jnp.where(places < fixed, places, shifted)]].set(jnp.asarray(sizes, jnp.int32))

    sizes = jnp.where(number % 4 == 0, named(heavy_load, number // 4), named(usual, number - number // 4 - 1))
    mixed = jax.random.permutation(jax.random.fold_in(own, 3), count)
    donor, taker = mixed[0:count // 2 * 2:2], mixed[1:count // 2 * 2:2]
    slack = jnp.minimum(sizes[donor] - 1, most - sizes[taker]) // 2
    slack = jnp.where((donor == ranking[0]) | (taker == ranking[0]) | (sizes[taker] == 0), 0, jnp.maximum(slack, 0))
    shifted = jax.random.randint(jax.random.fold_in(own, 4), (count // 2,), 0, 1 << 20) % (slack + 1)
    sizes = sizes.at[donor].add(-shifted).at[taker].add(shifted)
    members = jnp.searchsorted(jnp.cumsum(sizes), jnp.arange(rows * top), side="right").astype(jnp.int32)
    listing = members.reshape(top, rows).T
    listing = listing[jax.random.permutation(jax.random.fold_in(own, 1), rows)]
    offset_by = jax.random.randint(jax.random.fold_in(own, 2), (rows, 1), 0, top)
    return jnp.take_along_axis(listing, (jnp.arange(top)[None, :] + offset_by) % top, axis=1)


def shares(count, total, reach, lean, full):
    weights = [(1 << 20) // math.isqrt(grade ** lean) + 1 for grade in range(1, count + 1)]
    largest = reach if full else min(reach, max(-(-total // count), total * weights[0] // sum(weights)))
    least = 1 if total - largest >= count - 1 else 0
    given, spare = [largest] + [least] * (count - 1), total - largest - least * (count - 1)
    while spare > 0:
        free = [i for i in range(1, count) if given[i] < largest] or [i for i in range(1, count) if given[i] < reach]
        pool, remaining = sum([weights[i] for i in free]), spare
        for i in free:
            more = min(reach - given[i], max(1, remaining * weights[i] // pool), spare)
            given[i] = given[i] + more
            spare = spare - more
    return np.array(given)


def normal_values(key, dims, spread, limit, pieces=(), held_as=jnp.bfloat16):
    result = spread * jax.random.normal(key, dims, jnp.float32)
    if pieces:
        result = result * steps_of(key, dims, pieces, -0.22, 0.18)
    return jnp.clip(result, -limit, limit).astype(held_as)


def setup_inputs(seed: int = 0) -> dict:
    splits = jax.random.split(jax.random.key(seed), 6)
    tokens = normal_values(splits[0], (TOKENS, LATENT), 1.0, 6.0, ((0, 768),))
    cotangent = normal_values(splits[1], (TOKENS, LATENT), 1.0, 6.0, ((0, 768),))
    expert_ids_keys = jax.random.split(jax.random.fold_in(splits[2], 1), TOKENS // TOK_DEV)
    expert_ids_turns = jax.random.permutation(jax.random.fold_in(splits[2], 3), TOKENS // TOK_DEV)
    expert_ids = jax.vmap(lambda own, number: shared_out(jax.random.fold_in(splits[2], 2), own, number, TOK_DEV, EXPERTS, TOP_K, CAPACITY, 2))(expert_ids_keys, expert_ids_turns).reshape((TOKENS, TOP_K))
    route_weights = jnp.clip(0.099609375 + 0.9003906 * jax.random.uniform(splits[3], (TOKENS, TOP_K), jnp.float32) ** steps_of(splits[3], (TOKENS, TOP_K), ((0, 768),), -0.2, 0.2), 0.099609375, 1.0).astype(jnp.bfloat16)
    expert_weights = normal_values(splits[4], (EXPERTS, 3 * HIDDEN_SIZE, LATENT), LATENT ** -0.5, 0.1875, ((0, 8),))
    return dict(tokens=tokens, cotangent=cotangent, expert_ids=expert_ids, route_weights=route_weights, expert_weights=expert_weights)


def reference(tokens, cotangent, expert_ids, route_weights, expert_weights):
    total_slots = TOKENS * TOP_K
    most_rows = N_DP * N_EXPERT * CAPACITY
    flat_ids = expert_ids.reshape(total_slots)
    flat_weights = route_weights.reshape(total_slots)
    contract_last = (((1,), (1,)), ((), ()))
    contract_first = (((0,), (0,)), ((), ()))

    def per_expert(carry, expert):
        out_acc, grad_acc, route_acc = carry
        slot_index, = jnp.nonzero(flat_ids == expert, size=most_rows, fill_value=total_slots)
        slot_index = slot_index.astype(jnp.int32)
        present = slot_index < total_slots
        safe_index = jnp.where(present, slot_index, 0).astype(jnp.int32)
        token_index = (safe_index // TOP_K).astype(jnp.int32)
        x_rows = jnp.where(present[:, None], tokens[token_index], jnp.zeros((), tokens.dtype))
        cot_rows = jnp.where(present[:, None], cotangent[token_index], jnp.zeros((), cotangent.dtype))
        weight_rows = jnp.where(present, flat_weights[safe_index], jnp.zeros((), flat_weights.dtype))
        weights = expert_weights[expert]
        both = lax.dot_general(x_rows, weights[:2 * HIDDEN_SIZE], contract_last, preferred_element_type=jnp.float32)
        pre_gate = both[:, :HIDDEN_SIZE]
        pre_up = both[:, HIDDEN_SIZE:]
        sigmoid_gate = jax.nn.sigmoid(pre_gate)
        gate_act = pre_gate * sigmoid_gate
        hidden = (gate_act * pre_up).astype(jnp.bfloat16)
        slot_out = jnp.dot(hidden, weights[2 * HIDDEN_SIZE:], preferred_element_type=jnp.float32).astype(jnp.bfloat16)
        scaled = (weight_rows.astype(jnp.float32)[:, None] * cot_rows.astype(jnp.float32)).astype(jnp.bfloat16)
        hidden_grad = lax.dot_general(scaled, weights[2 * HIDDEN_SIZE:], contract_last, preferred_element_type=jnp.float32)
        up_grad = (hidden_grad * gate_act).astype(jnp.bfloat16)
        gate_grad = (hidden_grad * pre_up * sigmoid_gate * (1.0 + pre_gate * (1.0 - sigmoid_gate))).astype(jnp.bfloat16)
        both_grad = jnp.concatenate([gate_grad, up_grad], axis=1)
        slot_grad = jnp.dot(both_grad, weights[:2 * HIDDEN_SIZE], preferred_element_type=jnp.float32).astype(jnp.bfloat16)
        term = jnp.concatenate([lax.dot_general(both_grad, x_rows, contract_first, preferred_element_type=jnp.float32), lax.dot_general(hidden, scaled, contract_first, preferred_element_type=jnp.float32)], axis=0)
        out_f = slot_out.astype(jnp.float32)
        out_acc = out_acc.at[token_index].add(weight_rows.astype(jnp.float32)[:, None] * out_f)
        grad_acc = grad_acc.at[token_index].add(slot_grad.astype(jnp.float32))
        route_acc = route_acc.at[slot_index].add(lax.optimization_barrier(jnp.sum(cot_rows.astype(jnp.float32) * out_f, axis=1)))
        return ((out_acc, grad_acc, route_acc), term)
    start = (jnp.zeros((TOKENS, LATENT), jnp.float32), jnp.zeros((TOKENS, LATENT), jnp.float32), jnp.zeros((total_slots + 1,), jnp.float32))
    (out_acc, grad_acc, route_acc), terms = lax.scan(per_expert, start, jnp.arange(EXPERTS, dtype=jnp.int32))
    factor = 1.0 / math.sqrt(TOKENS)
    return (out_acc.astype(jnp.bfloat16), grad_acc.astype(jnp.bfloat16), route_acc[:total_slots].reshape(TOKENS, TOP_K), terms * factor)
```

```python
import math

import jax
import jax.numpy as jnp
from jax import lax
from jax.experimental import pallas as pl
from jax.experimental.pallas import tpu as pltpu
from jax.sharding import PartitionSpec as P

MESH = pl.DeviceIdType.MESH
F32 = jnp.float32
BF16 = jnp.bfloat16

HID = 512
CAP = 64
NX = 4
NY = 8
COLS_A = 512
SUBS = 2

NT = (((1,), (1,)), ((), ()))
TN = (((0,), (0,)), ((), ()))


def dot(a, b, dims=(((1,), (0,)), ((), ()))):
    return lax.dot_general(a, b, dims, preferred_element_type=F32)


class Messages:
    def __init__(self, send_sems, recv_sems):
        self.send_sems, self.recv_sems, self.all = send_sems, recv_sems, []

    def start(self, src, dst, device):
        i = len(self.all)
        copy = pltpu.make_async_remote_copy(
            src_ref=src,
            dst_ref=dst,
            send_sem=self.send_sems.at[i],
            recv_sem=self.recv_sems.at[i],
            device_id=device,
            device_id_type=MESH,
        )
        copy.start()
        self.all.append(copy)
        return copy


class Chain:
    def __init__(self, net, pos, n, left, right, term, bufs):
        self.net, self.pos, self.n, self.left, self.right, self.term = net, pos, n, left, right, term
        self.send_r, self.recv_r, self.send_l, self.recv_l = bufs
        self.hr, self.hl = n // 2, n - 1 - n // 2
        self.mr, self.ml = [], []

    def step(self, s):
        if s < self.hr:
            v = self.term(lax.rem(self.pos + self.hr - s, self.n))
            if s:
                self.mr[s - 1].wait_recv()
                v = v + self.recv_r[s - 1].astype(F32)
            self.send_r[s] = v.astype(BF16)
            self.mr.append(self.net.start(self.send_r.at[s], self.recv_r.at[s], self.right))
        if s < self.hl:
            v = self.term(lax.rem(self.pos + self.n - self.hl + s, self.n))
            if s:
                self.ml[s - 1].wait_recv()
                v = v + self.recv_l[s - 1].astype(F32)
            self.send_l[s] = v.astype(BF16)
            self.ml.append(self.net.start(self.send_l.at[s], self.recv_l.at[s], self.left))

    def final(self):
        v = self.term(self.pos)
        self.mr[self.hr - 1].wait_recv()
        v = v + self.recv_r[self.hr - 1].astype(F32)
        if self.hl:
            self.ml[self.hl - 1].wait_recv()
            v = v + self.recv_l[self.hl - 1].astype(F32)
        return v


def kernel(
    nz, factor,
    tok, cot, ids, wts, ew,
    lat_o, tg_o, rg_o, eg_o,
    weights, tok_b, cot_b, route_b, pick_b, rhs_b, cot_s, grad_s,
    con_l, con_g, sib_l, sib_g, part_l, part_g, xin, rg_s, rg_r,
    term_b, asr, arr, asl, arl, bsr, brr, bsl, brl, sum_a, sum_b, two_a, two_b, in_a, in_b,
    local_sem, send_sems, recv_sems,
):
    dp, ex = lax.axis_index("dp"), lax.axis_index("expert")
    z, y = lax.div(dp, NY), lax.rem(dp, NY)
    x, c = lax.div(ex, 2), lax.rem(ex, 2)

    def in_group(dx, dc):
        return {"dp": dp, "expert": lax.rem(x + dx + NX, NX) * 2 + lax.rem(c + dc, 2)}

    def along_y(d):
        return {"dp": z * NY + lax.rem(y + d + NY, NY), "expert": ex}

    def along_z(d):
        return {"dp": lax.rem(z + d + nz, nz) * NY + y, "expert": ex}

    offset = (0, -1, 1, 2)
    inverse = (0, 2, 1, 3)

    load = pltpu.make_async_copy(ew, weights, local_sem)
    load.start()
    expert_of = lax.broadcasted_iota(jnp.int32, (8, 128), 0)
    w_in = wts[...].astype(F32)
    id_in = ids[...]
    route_b[0] = sum(
        jnp.where(id_in[k : k + 1] == expert_of, w_in[k : k + 1], 0.0) for k in range(2)
    )

    barrier = pltpu.get_barrier_semaphore()
    partners = (
        [in_group(offset[k % 4], k // 4) for k in range(1, 8)]
        + [along_y(d) for d in range(1, NY)]
        + [along_z(d) for d in range(1, nz)]
    )
    for device in partners:
        pl.semaphore_signal(barrier, inc=1, device_id=device, device_id_type=MESH)
    pl.semaphore_wait(barrier, len(partners))

    net = Messages(send_sems, recv_sems)
    right, left, sibling = in_group(1, 0), in_group(-1, 0), in_group(0, 1)

    route_in = [
        net.start(route_b.at[0], route_b.at[inverse[k % 4] + k // 4 * 4], in_group(offset[k % 4], k // 4))
        for k in range(1, 8)
    ]
    sib_t, sib_c = [None] * 4, [None] * 4
    tok_l = net.start(tok, tok_b.at[0], right)
    cot_r = net.start(cot, cot_b.at[1], left)
    sib_t[0] = net.start(tok, tok_b.at[3], sibling)
    sib_c[0] = net.start(cot, cot_b.at[3], sibling)
    cot_l = net.start(cot, cot_b.at[0], right)
    tok_r = net.start(tok, tok_b.at[1], left)

    def block(k):
        return (tok, cot) if k == 0 else (tok_b.at[k - 1], cot_b.at[k - 1])

    for m in route_in:
        m.wait_recv()
    rows = jnp.concatenate([route_b[k, pl.ds(ex, 1), :] for k in range(8)], axis=0)
    before = (
        lax.broadcasted_iota(jnp.int32, (128, 128), 0) < lax.broadcasted_iota(jnp.int32, (128, 128), 1)
    ).astype(F32)
    ranks = dot(jnp.where(rows > 0, 1.0, 0.0).astype(BF16), before.astype(BF16))
    seat = lax.broadcasted_iota(jnp.int32, (CAP, 128), 0).astype(F32)
    load.wait()

    def stage(slots, base):
        size = CAP * len(slots)
        own = pl.ds(base, size)
        w_of = []
        for i, k in enumerate(slots):
            at = pl.ds(base + CAP * i, CAP)
            pick = jnp.where((ranks[k : k + 1] == seat) & (rows[k : k + 1] > 0), 1.0, 0.0)
            w = jnp.sum(pick * rows[k : k + 1], axis=1, keepdims=True)
            w_of.append(w)
            pick = pick.astype(BF16)
            pick_b[k] = pick
            t_ref, c_ref = block(k)
            rhs_b[0, at, :] = dot(pick, t_ref[...]).astype(BF16)
            cots = dot(pick, c_ref[...])
            cot_s[at, :] = cots.astype(BF16)
            rhs_b[1, at, :] = (w * cots).astype(BF16)
        w = jnp.concatenate(w_of, axis=0)
        both = dot(rhs_b[0, own, :], weights[: 2 * HID, :], NT)
        gate, up = both[:, :HID], both[:, HID:]
        sig = 1.0 / (1.0 + jnp.exp(-gate))
        act = gate * sig
        hidden = (act * up).astype(BF16)
        grad_s[own, 2 * HID :] = hidden
        d_hidden = dot(rhs_b[1, own, :], weights[2 * HID :, :], NT)
        grad_s[own, HID : 2 * HID] = (d_hidden * act).astype(BF16)
        grad_s[own, :HID] = (d_hidden * up * sig * (1.0 + gate * (1.0 - sig))).astype(BF16)
        out = dot(hidden, weights[2 * HID :, :]).astype(BF16).astype(F32)
        r_grad = jnp.sum(cot_s[own, :].astype(F32) * out, axis=1, keepdims=True)
        out = (w * out).astype(BF16)
        d_x = dot(grad_s[own, : 2 * HID], weights[: 2 * HID, :]).astype(BF16)
        for i, k in enumerate(slots):
            pick = pick_b[k]
            part = slice(CAP * i, CAP * (i + 1))
            con_l[k] = dot(pick, out[part], TN).astype(BF16)
            con_g[k] = dot(pick, d_x[part], TN).astype(BF16)
            line = jnp.sum(pick.astype(F32) * r_grad[part], axis=0, keepdims=True)
            rg_s[k] = jnp.broadcast_to(line, (8, 128))

    sib_out = {}

    def to_sibling(k):
        sib_out[k] = (
            net.start(con_l.at[k + 4], sib_l.at[k], sibling),
            net.start(con_g.at[k + 4], sib_g.at[k], sibling),
        )

    def chip_part(k):
        for m in sib_out[k]:
            m.wait_recv()
        part_l[k] = (con_l[k].astype(F32) + sib_l[k].astype(F32)).astype(BF16)
        part_g[k] = (con_g[k].astype(F32) + sib_g[k].astype(F32)).astype(BF16)

    sib_t[0].wait_recv()
    sib_c[0].wait_recv()
    stage((0, 4), 0)
    to_sibling(0)

    tok_l.wait_recv()
    opp_t = net.start(tok_b.at[0], tok_b.at[2], right)
    sib_t[1] = net.start(tok_b.at[0], tok_b.at[4], sibling)
    cot_r.wait_recv()
    opp_c = net.start(cot_b.at[1], cot_b.at[2], left)
    sib_c[2] = net.start(cot_b.at[1], cot_b.at[5], sibling)
    cot_l.wait_recv()
    sib_c[1] = net.start(cot_b.at[0], cot_b.at[4], sibling)
    tok_r.wait_recv()
    sib_t[2] = net.start(tok_b.at[1], tok_b.at[5], sibling)
    for k in (1, 2):
        sib_t[k].wait_recv()
        sib_c[k].wait_recv()
    stage((1, 2, 5, 6), 2 * CAP)
    to_sibling(1)
    to_sibling(2)
    opp_t.wait_recv()
    sib_t[3] = net.start(tok_b.at[2], tok_b.at[6], sibling)
    opp_c.wait_recv()
    sib_c[3] = net.start(cot_b.at[2], cot_b.at[6], sibling)
    chip_part(1)
    chip_part(2)
    near_g = net.start(part_g.at[2], xin.at[0], right)
    near_l = net.start(part_l.at[1], xin.at[1], left)
    sib_t[3].wait_recv()
    sib_c[3].wait_recv()
    stage((3, 7), 6 * CAP)
    to_sibling(3)

    def term_of(i, carry):
        at = pl.multiple_of(i * 128, 128)
        t = dot(grad_s[:, pl.ds(at, 128)], rhs_b[lax.div(at, 2 * HID)], TN)
        term_b[i] = t.reshape(NY, 16, t.shape[1])
        return carry

    lax.fori_loop(0, nz, term_of, 0)

    wide_a, wide_b = asr.shape[-1], bsr.shape[-1]

    def chain_a(q):
        def term(t):
            return term_b[:, t, :, q * wide_a : (q + 1) * wide_a]

        bufs = [b.at[q] for b in (asr, arr, asl, arl)]
        return Chain(net, y, NY, along_y(-1), along_y(1), term, bufs)

    def chain_b(q):
        def term(t):
            return term_b[t, :, :, COLS_A + q * wide_b : COLS_A + (q + 1) * wide_b]

        bufs = [b.at[q] for b in (bsr, brr, bsl, brl)]
        return Chain(net, z, nz, along_z(-1), along_z(1), term, bufs)

    chains_a = [chain_a(q) for q in range(SUBS)]
    chains_b = [chain_b(q) for q in range(SUBS)]

    def ring(s):
        for q in range(SUBS):
            chains_a[q].step(s)
            chains_b[q].step(s)

    ring(0)
    chip_part(3)
    far_l = net.start(part_l.at[3], xin.at[2], right)
    far_g = net.start(part_g.at[3], xin.at[3], left)
    rg_in = [
        net.start(rg_s.at[k], rg_r.at[inverse[k % 4] + k // 4 * 4], in_group(offset[k % 4], k // 4))
        for k in range(1, 8)
    ]
    ring(1)
    ring(2)
    far_l.wait_recv()
    part_l[2] = (part_l[2].astype(F32) + xin[2].astype(F32)).astype(BF16)
    last_l = net.start(part_l.at[2], xin.at[4], right)
    far_g.wait_recv()
    part_g[1] = (part_g[1].astype(F32) + xin[3].astype(F32)).astype(BF16)
    last_g = net.start(part_g.at[1], xin.at[5], left)
    ring(3)
    chip_part(0)
    for q in range(SUBS):
        sum_a[:, :, q * wide_a : (q + 1) * wide_a] = chains_a[q].final()
    two_a[...] = sum_a[...].astype(BF16)
    a_in = [
        net.start(two_a.at[lax.rem(z + d, nz)], in_a.at[d - 1], along_z(d)) for d in range(1, nz)
    ]
    for s in range(4, nz // 2):
        ring(s)
    for q in range(SUBS):
        sum_b[:, :, q * wide_b : (q + 1) * wide_b] = chains_b[q].final()
    two_b[...] = sum_b[...].astype(BF16)
    b_in = [
        net.start(two_b.at[lax.rem(y + d, NY)], in_b.at[d - 1], along_y(d)) for d in range(1, NY)
    ]

    near_g.wait_recv()
    last_g.wait_recv()
    tg_o[...] = (part_g[0].astype(F32) + xin[0].astype(F32) + xin[5].astype(F32)).astype(BF16)
    near_l.wait_recv()
    last_l.wait_recv()
    lat_o[...] = (part_l[0].astype(F32) + xin[1].astype(F32) + xin[4].astype(F32)).astype(BF16)
    route = [jnp.zeros((1, 128), F32), jnp.zeros((1, 128), F32)]
    for m in rg_in:
        m.wait_recv()
    for k in range(8):
        line = rg_s[0, 0:1, :] if k == 0 else rg_r[k, 0:1, :]
        expert = in_group(offset[k % 4], k // 4)["expert"]
        for j in range(2):
            route[j] = route[j] + jnp.where(id_in[j : j + 1] == expert, line, 0.0)
    rg_o[...] = jnp.concatenate(route, axis=0)

    for m in a_in:
        m.wait_recv()
    eg_o[:, :COLS_A] = factor * (sum_a[z] + jnp.sum(in_a[...].astype(F32), axis=0))
    for m in b_in:
        m.wait_recv()
    eg_o[:, COLS_A:] = factor * (sum_b[y] + jnp.sum(in_b[...].astype(F32), axis=0))
    for m in net.all:
        m.wait_send()


def solution(mesh):
    n_dp, n_ex = mesh.shape["dp"], mesh.shape["expert"]
    nz = n_dp // NY

    def body(tokens, cotangent, expert_ids, route_weights, expert_weights):
        count, width = tokens.shape
        slots = CAP * n_ex
        factor = 1.0 / math.sqrt(count * n_dp * n_ex)
        wide_a, wide_b = COLS_A // SUBS, (width - COLS_A) // SUBS
        hr_a, hl_a = NY // 2, NY - 1 - NY // 2
        hr_b, hl_b = nz // 2, nz - 1 - nz // 2
        vmem = pl.BlockSpec(memory_space=pltpu.VMEM)
        count_messages = 7 + 6 + 6 + 2 + 8 + 6 + 7 + SUBS * (NY - 1 + nz - 1) + nz - 1 + NY - 1
        lat, tg, rg, eg = pl.pallas_call(
            lambda *refs: kernel(nz, factor, *refs),
            out_shape=(
                jax.ShapeDtypeStruct((count, width), BF16),
                jax.ShapeDtypeStruct((count, width), BF16),
                jax.ShapeDtypeStruct((2, count), F32),
                jax.ShapeDtypeStruct((16, width), F32),
            ),
            in_specs=[vmem, vmem, vmem, vmem, pl.BlockSpec(memory_space=pl.ANY)],
            out_specs=(vmem,) * 4,
            scratch_shapes=[
                pltpu.VMEM((3 * HID, width), BF16),
                pltpu.VMEM((7, count, width), BF16),
                pltpu.VMEM((7, count, width), BF16),
                pltpu.VMEM((8, 8, 128), F32),
                pltpu.VMEM((8, CAP, 128), BF16),
                pltpu.VMEM((2, slots, width), BF16),
                pltpu.VMEM((slots, width), BF16),
                pltpu.VMEM((slots, 3 * HID), BF16),
                pltpu.VMEM((8, count, width), BF16),
                pltpu.VMEM((8, count, width), BF16),
                pltpu.VMEM((4, count, width), BF16),
                pltpu.VMEM((4, count, width), BF16),
                pltpu.VMEM((4, count, width), BF16),
                pltpu.VMEM((4, count, width), BF16),
                pltpu.VMEM((6, count, width), BF16),
                pltpu.VMEM((8, 8, 128), F32),
                pltpu.VMEM((8, 8, 128), F32),
                pltpu.VMEM((nz, NY, 16, width), F32),
                pltpu.VMEM((SUBS, hr_a, nz, 16, wide_a), BF16),
                pltpu.VMEM((SUBS, hr_a, nz, 16, wide_a), BF16),
                pltpu.VMEM((SUBS, hl_a, nz, 16, wide_a), BF16),
                pltpu.VMEM((SUBS, hl_a, nz, 16, wide_a), BF16),
                pltpu.VMEM((SUBS, hr_b, NY, 16, wide_b), BF16),
                pltpu.VMEM((SUBS, hr_b, NY, 16, wide_b), BF16),
                pltpu.VMEM((SUBS, hl_b, NY, 16, wide_b), BF16),
                pltpu.VMEM((SUBS, hl_b, NY, 16, wide_b), BF16),
                pltpu.VMEM((nz, 16, COLS_A), F32),
                pltpu.VMEM((NY, 16, width - COLS_A), F32),
                pltpu.VMEM((nz, 16, COLS_A), BF16),
                pltpu.VMEM((NY, 16, width - COLS_A), BF16),
                pltpu.VMEM((nz - 1, 16, COLS_A), BF16),
                pltpu.VMEM((NY - 1, 16, width - COLS_A), BF16),
                pltpu.SemaphoreType.DMA,
                pltpu.SemaphoreType.DMA((count_messages,)),
                pltpu.SemaphoreType.DMA((count_messages,)),
            ],
            compiler_params=pltpu.CompilerParams(
                collective_id=0, has_side_effects=True, vmem_limit_bytes=60 * 1024 * 1024
            ),
        )(
            tokens,
            cotangent,
            expert_ids.T,
            route_weights.T,
            expert_weights.reshape(expert_weights.shape[1:]),
        )
        return lat, tg, rg.T, eg[None]

    return jax.shard_map(
        body,
        mesh=mesh,
        in_specs=(
            P(("dp", "expert"), None),
            P(("dp", "expert"), None),
            P(("dp", "expert"), None),
            P(("dp", "expert"), None),
            P("expert", None, None),
        ),
        out_specs=(
            P(("dp", "expert"), None),
            P(("dp", "expert"), None),
            P(("dp", "expert"), None),
            P("expert", "dp", None),
        ),
        check_vma=False,
    )
```

```python
import math

import jax
import jax.numpy as jnp
from jax import lax
from jax.experimental import pallas as pl
from jax.experimental.pallas import tpu as pltpu
from jax.sharding import PartitionSpec as P

MESH = pl.DeviceIdType.MESH
F32 = jnp.float32
BF16 = jnp.bfloat16

HID = 512
CAP = 64
NX = 4
NY = 8
WIDE = 128
CHAINS_A = 4
COLS_A = CHAINS_A * WIDE
PARTS = 2
TIME_A, TIME_B = 4.6, 3.3

NT = (((1,), (1,)), ((), ()))
TN = (((0,), (0,)), ((), ()))


def dot(a, b, dims=(((1,), (0,)), ((), ()))):
    return lax.dot_general(a, b, dims, preferred_element_type=F32)


class Message:
    def __init__(self, copy):
        self.copy, self.got = copy, False

    def wait_recv(self):
        assert not self.got
        self.got = True
        self.copy.wait_recv()


class Messages:
    def __init__(self, send_sems, recv_sems):
        self.send_sems, self.recv_sems, self.all = send_sems, recv_sems, []

    def start(self, src, dst, device):
        i = len(self.all)
        copy = pltpu.make_async_remote_copy(
            src_ref=src,
            dst_ref=dst,
            send_sem=self.send_sems.at[i],
            recv_sem=self.recv_sems.at[i],
            device_id=device,
            device_id_type=MESH,
        )
        copy.start()
        message = Message(copy)
        self.all.append(message)
        return message


class Chain:
    def __init__(self, net, pos, n, sign, along, term, bufs):
        self.net, self.pos, self.n, self.sign, self.term = net, pos, n, sign, term
        self.far, self.near = n // 2, n - 1 - n // 2
        send_f, recv_f, send_n, recv_n = bufs
        self.ways = (
            (sign, self.far, along(sign), send_f, recv_f, []),
            (-sign, self.near, along(-sign), send_n, recv_n, []),
        )

    def step(self, s):
        for sign, hops, device, send, recv, sent in self.ways:
            if s >= hops:
                continue
            v = self.term(lax.rem(self.pos + self.n + sign * (hops - s), self.n))
            if s:
                sent[s - 1].wait_recv()
                v = v + recv[s - 1].astype(F32)
            send[s] = v.astype(BF16)
            sent.append(self.net.start(send.at[s], recv.at[s], device))

    def final(self):
        v = self.term(self.pos)
        for sign, hops, device, send, recv, sent in self.ways:
            sent[hops - 1].wait_recv()
            v = v + recv[hops - 1].astype(F32)
        return v


def kernel(
    nz, factor,
    tok_h, cot_h, ids_h, wts_h, ew,
    lat_o, tg_o, rg_o, eg_o,
    tok, cot, ids, wts, weights, tok_b, cot_b, route_b, pick_b, rhs_b, cot_s, grad_s,
    con_l, con_g, sib_l, sib_g, part_l, part_g, xin, rg_s, rg_r,
    term_b, asr, arr, asl, arl, bsr, brr, bsl, brl, sum_a, sum_b, two_a, two_b, in_a, in_b,
    local_sems, send_sems, recv_sems,
):
    dp, ex = lax.axis_index("dp"), lax.axis_index("expert")
    z, y = lax.div(dp, NY), lax.rem(dp, NY)
    x, c = lax.div(ex, 2), lax.rem(ex, 2)

    def in_group(dx, dc):
        return {"dp": dp, "expert": lax.rem(x + dx + NX, NX) * 2 + lax.rem(c + dc, 2)}

    def along_y(d):
        return {"dp": z * NY + lax.rem(y + d + NY, NY), "expert": ex}

    def along_z(d):
        return {"dp": lax.rem(z + d + nz, nz) * NY + y, "expert": ex}

    offset = (0, -1, 1, 2)
    inverse = (0, 2, 1, 3)

    loads = [
        pltpu.make_async_copy(src, dst, local_sems.at[i])
        for i, (src, dst) in enumerate(
            ((ids_h, ids), (wts_h, wts), (tok_h, tok), (cot_h, cot), (ew, weights))
        )
    ]
    for load in loads:
        load.start()
    barrier = pltpu.get_barrier_semaphore()
    partners = (
        [in_group(offset[k % 4], k // 4) for k in range(1, 8)]
        + [along_y(d) for d in range(1, NY)]
        + [along_z(d) for d in range(1, nz)]
    )
    for device in partners:
        pl.semaphore_signal(barrier, inc=1, device_id=device, device_id_type=MESH)
    for load in loads[:2]:
        load.wait()
    expert_of = lax.broadcasted_iota(jnp.int32, (8, 128), 0)
    w_in = wts[...].astype(F32)
    id_in = ids[...]
    route_b[0] = sum(
        jnp.where(id_in[k : k + 1] == expert_of, w_in[k : k + 1], 0.0) for k in range(2)
    )
    for load in loads[2:4]:
        load.wait()
    pl.semaphore_wait(barrier, len(partners))

    net = Messages(send_sems, recv_sems)
    right, left, sibling = in_group(1, 0), in_group(-1, 0), in_group(0, 1)

    route_in = [
        net.start(route_b.at[0], route_b.at[inverse[k % 4] + k // 4 * 4], in_group(offset[k % 4], k // 4))
        for k in range(1, 8)
    ]
    sib_t, sib_c = [None] * 4, [None] * 4
    tok_l = net.start(tok, tok_b.at[0], right)
    cot_r = net.start(cot, cot_b.at[1], left)
    sib_t[0] = net.start(tok, tok_b.at[3], sibling)
    sib_c[0] = net.start(cot, cot_b.at[3], sibling)
    cot_l = net.start(cot, cot_b.at[0], right)
    tok_r = net.start(tok, tok_b.at[1], left)

    def done():
        for m in net.all:
            if not m.got:
                m.wait_recv()
            m.copy.wait_send()

    def block(k):
        return (tok, cot) if k == 0 else (tok_b.at[k - 1], cot_b.at[k - 1])

    for m in route_in:
        m.wait_recv()
    rows = jnp.concatenate([route_b[k, pl.ds(ex, 1), :] for k in range(8)], axis=0)
    before = (
        lax.broadcasted_iota(jnp.int32, (128, 128), 0) < lax.broadcasted_iota(jnp.int32, (128, 128), 1)
    ).astype(F32)
    ranks = dot(jnp.where(rows > 0, 1.0, 0.0).astype(BF16), before.astype(BF16))
    seat = lax.broadcasted_iota(jnp.int32, (CAP, 128), 0).astype(F32)
    loads[4].wait()

    def stage(slots, base):
        size = CAP * len(slots)
        own = pl.ds(base, size)
        w_of = []
        for i, k in enumerate(slots):
            at = pl.ds(base + CAP * i, CAP)
            pick = jnp.where((ranks[k : k + 1] == seat) & (rows[k : k + 1] > 0), 1.0, 0.0)
            w = jnp.sum(pick * rows[k : k + 1], axis=1, keepdims=True)
            w_of.append(w)
            pick = pick.astype(BF16)
            pick_b[k] = pick
            t_ref, c_ref = block(k)
            rhs_b[0, at, :] = dot(pick, t_ref[...]).astype(BF16)
            cots = dot(pick, c_ref[...])
            cot_s[at, :] = cots.astype(BF16)
            rhs_b[1, at, :] = (w * cots).astype(BF16)
        w = jnp.concatenate(w_of, axis=0)
        both = dot(rhs_b[0, own, :], weights[: 2 * HID, :], NT)
        gate, up = both[:, :HID], both[:, HID:]
        sig = 1.0 / (1.0 + jnp.exp(-gate))
        act = gate * sig
        hidden = (act * up).astype(BF16)
        grad_s[own, 2 * HID :] = hidden
        d_hidden = dot(rhs_b[1, own, :], weights[2 * HID :, :], NT)
        grad_s[own, HID : 2 * HID] = (d_hidden * act).astype(BF16)
        grad_s[own, :HID] = (d_hidden * up * sig * (1.0 + gate * (1.0 - sig))).astype(BF16)
        out = dot(hidden, weights[2 * HID :, :]).astype(BF16).astype(F32)
        r_grad = jnp.sum(cot_s[own, :].astype(F32) * out, axis=1, keepdims=True)
        out = (w * out).astype(BF16)
        d_x = dot(grad_s[own, : 2 * HID], weights[: 2 * HID, :]).astype(BF16)
        for i, k in enumerate(slots):
            pick = pick_b[k]
            part = slice(CAP * i, CAP * (i + 1))
            con_l[k] = dot(pick, out[part], TN).astype(BF16)
            con_g[k] = dot(pick, d_x[part], TN).astype(BF16)
            line = jnp.sum(pick.astype(F32) * r_grad[part], axis=0, keepdims=True)
            rg_s[k] = jnp.broadcast_to(line, (8, 128))

    sib_out = {}

    def to_sibling(k):
        sib_out[k] = (
            net.start(con_l.at[k + 4], sib_l.at[k], sibling),
            net.start(con_g.at[k + 4], sib_g.at[k], sibling),
        )

    def chip_part(k):
        for m in sib_out[k]:
            m.wait_recv()
        part_l[k] = (con_l[k].astype(F32) + sib_l[k].astype(F32)).astype(BF16)
        part_g[k] = (con_g[k].astype(F32) + sib_g[k].astype(F32)).astype(BF16)

    sib_t[0].wait_recv()
    sib_c[0].wait_recv()
    stage((0, 4), 0)
    to_sibling(0)

    tok_l.wait_recv()
    opp_t = net.start(tok_b.at[0], tok_b.at[2], right)
    sib_t[1] = net.start(tok_b.at[0], tok_b.at[4], sibling)
    cot_r.wait_recv()
    opp_c = net.start(cot_b.at[1], cot_b.at[2], left)
    sib_c[2] = net.start(cot_b.at[1], cot_b.at[5], sibling)
    cot_l.wait_recv()
    sib_c[1] = net.start(cot_b.at[0], cot_b.at[4], sibling)
    tok_r.wait_recv()
    sib_t[2] = net.start(tok_b.at[1], tok_b.at[5], sibling)
    for k in (1, 2):
        sib_t[k].wait_recv()
        sib_c[k].wait_recv()
    stage((1, 2, 5, 6), 2 * CAP)
    to_sibling(1)
    to_sibling(2)
    opp_t.wait_recv()
    sib_t[3] = net.start(tok_b.at[2], tok_b.at[6], sibling)
    opp_c.wait_recv()
    sib_c[3] = net.start(cot_b.at[2], cot_b.at[6], sibling)
    chip_part(1)
    chip_part(2)
    near_g = net.start(part_g.at[2], xin.at[0], right)
    near_l = net.start(part_l.at[1], xin.at[1], left)
    sib_t[3].wait_recv()
    sib_c[3].wait_recv()
    stage((3, 7), 6 * CAP)
    to_sibling(3)

    def term_of(low, high):
        def some_rows(i, carry):
            at = pl.multiple_of(i * 128, 128)
            t = dot(grad_s[:, pl.ds(at, 128)], rhs_b[lax.div(at, 2 * HID), :, low:high], TN)
            term_b[i, :, :, low:high] = t.reshape(NY, 16, high - low)
            return carry

        lax.fori_loop(0, nz, some_rows, 0)

    chains_b = term_b.shape[-1] // WIDE - CHAINS_A

    def chain_a(q):
        def term(t):
            return term_b[:, t, :, q * WIDE : (q + 1) * WIDE]

        bufs = [b.at[q] for b in (asr, arr, asl, arl)]
        return Chain(net, y, NY, 1 - q % 2 * 2, along_y, term, bufs)

    def chain_b(q):
        def term(t):
            return term_b[t, :, :, COLS_A + q * WIDE : COLS_A + (q + 1) * WIDE]

        bufs = [b.at[q] for b in (bsr, brr, bsl, brl)]
        return Chain(net, z, nz, 1 - q % 2 * 2, along_z, term, bufs)

    def far_parts():
        chip_part(3)
        relay["far_l"] = net.start(part_l.at[3], xin.at[2], right)
        relay["far_g"] = net.start(part_g.at[3], xin.at[3], left)
        relay["route"] = [
            net.start(rg_s.at[k], rg_r.at[inverse[k % 4] + k // 4 * 4], in_group(offset[k % 4], k // 4))
            for k in range(1, 8)
        ]

    def last_parts():
        relay["far_l"].wait_recv()
        part_l[2] = (part_l[2].astype(F32) + xin[2].astype(F32)).astype(BF16)
        relay["last_l"] = net.start(part_l.at[2], xin.at[4], right)
        relay["far_g"].wait_recv()
        part_g[1] = (part_g[1].astype(F32) + xin[3].astype(F32)).astype(BF16)
        relay["last_g"] = net.start(part_g.at[1], xin.at[5], left)
        chip_part(0)

    def final_a(q):
        v = all_a[q].final()
        sum_a[:, :, q * WIDE : (q + 1) * WIDE] = v
        two_a[:, :, q * WIDE : (q + 1) * WIDE] = v.astype(BF16)

    def final_b(q):
        v = all_b[q].final()
        sum_b[:, :, q * WIDE : (q + 1) * WIDE] = v
        two_b[:, :, q * WIDE : (q + 1) * WIDE] = v.astype(BF16)

    def farthest_first(n):
        return sorted(range(1, n), key=lambda d: -min(d, n - d))

    def second_a(i):
        cols = slice(i * COLS_A // PARTS, (i + 1) * COLS_A // PARTS)
        a_in.extend(
            net.start(two_a.at[lax.rem(z + d, nz), :, cols], in_a.at[d - 1, :, cols], along_z(d))
            for d in farthest_first(nz)
        )

    def second_b(i):
        wide = two_b.shape[-1]
        cols = slice(i * wide // PARTS, (i + 1) * wide // PARTS)
        b_in.extend(
            net.start(two_b.at[lax.rem(y + d, NY), :, cols], in_b.at[d - 1, :, cols], along_y(d))
            for d in farthest_first(NY)
        )

    a_in, b_in = [], []
    relay = {}
    all_a = [chain_a(q) for q in range(CHAINS_A)]
    all_b = [chain_b(q) for q in range(chains_b)]
    term_of(0, COLS_A)
    for q in range(CHAINS_A):
        all_a[q].step(0)
    term_of(COLS_A, term_b.shape[-1])
    for q in range(chains_b):
        all_b[q].step(0)
    events = [(0.0, far_parts), (2.5 * TIME_A, last_parts)]
    for q in range(CHAINS_A):
        for s in range(1, NY // 2):
            events.append(((s + q / CHAINS_A) * TIME_A, lambda q=q, s=s: all_a[q].step(s)))
        events.append(((NY // 2 + q / CHAINS_A) * TIME_A, lambda q=q: final_a(q)))
    for q in range(chains_b):
        for s in range(1, nz // 2):
            events.append(((s + q / chains_b) * TIME_B, lambda q=q, s=s: all_b[q].step(s)))
        events.append(((nz // 2 + q / chains_b) * TIME_B, lambda q=q: final_b(q)))
    for i in range(PARTS):
        last = (i + 1) * CHAINS_A // PARTS - 1
        at = (NY // 2 + last / CHAINS_A) * TIME_A
        events.append((at + 0.01, lambda i=i: second_a(i)))
        last = (i + 1) * chains_b // PARTS - 1
        at = (nz // 2 + last / chains_b) * TIME_B
        events.append((at + 0.01, lambda i=i: second_b(i)))
    for _, event in sorted(events, key=lambda e: e[0]):
        event()
    rg_in = relay["route"]

    near_g.wait_recv()
    relay["last_g"].wait_recv()
    tg_o[...] = (part_g[0].astype(F32) + xin[0].astype(F32) + xin[5].astype(F32)).astype(BF16)
    near_l.wait_recv()
    relay["last_l"].wait_recv()
    lat_o[...] = (part_l[0].astype(F32) + xin[1].astype(F32) + xin[4].astype(F32)).astype(BF16)
    route = [jnp.zeros((1, 128), F32), jnp.zeros((1, 128), F32)]
    for m in rg_in:
        m.wait_recv()
    for k in range(8):
        line = rg_s[0, 0:1, :] if k == 0 else rg_r[k, 0:1, :]
        expert = in_group(offset[k % 4], k // 4)["expert"]
        for j in range(2):
            route[j] = route[j] + jnp.where(id_in[j : j + 1] == expert, line, 0.0)
    rg_o[...] = jnp.concatenate(route, axis=0)

    for m in a_in:
        m.wait_recv()
    eg_o[:, :COLS_A] = factor * (sum_a[z] + jnp.sum(in_a[...].astype(F32), axis=0))
    for m in b_in:
        m.wait_recv()
    eg_o[:, COLS_A:] = factor * (sum_b[y] + jnp.sum(in_b[...].astype(F32), axis=0))
    done()


def pass_on(*refs):
    for i in range(4):
        refs[4 + i][...] = refs[i][...]


def solution(mesh):
    n_dp, n_ex = mesh.shape["dp"], mesh.shape["expert"]
    nz = n_dp // NY

    def body(tokens, cotangent, expert_ids, route_weights, expert_weights):
        count, width = tokens.shape
        slots = CAP * n_ex
        factor = 1.0 / math.sqrt(count * n_dp * n_ex)
        chains_a, chains_b = CHAINS_A, width // WIDE - CHAINS_A
        hr_a, hl_a = NY // 2, NY - 1 - NY // 2
        hr_b, hl_b = nz // 2, nz - 1 - nz // 2
        vmem = pl.BlockSpec(memory_space=pltpu.VMEM)
        count_messages = 7 + 6 + 6 + 2 + 8 + 6 + 7 + chains_a * (NY - 1) + chains_b * (nz - 1) + PARTS * (nz - 1 + NY - 1)
        lat, tg, rg, eg = pl.pallas_call(
            lambda *refs: kernel(nz, factor, *refs),
            out_shape=(
                jax.ShapeDtypeStruct((count, width), BF16),
                jax.ShapeDtypeStruct((count, width), BF16),
                jax.ShapeDtypeStruct((2, count), F32),
                jax.ShapeDtypeStruct((16, width), F32),
            ),
            in_specs=[pl.BlockSpec(memory_space=pltpu.HBM)] * 5,
            out_specs=(vmem,) * 4,
            scratch_shapes=[
                pltpu.VMEM((count, width), BF16),
                pltpu.VMEM((count, width), BF16),
                pltpu.VMEM((2, count), jnp.int32),
                pltpu.VMEM((2, count), BF16),
                pltpu.VMEM((3 * HID, width), BF16),
                pltpu.VMEM((7, count, width), BF16),
                pltpu.VMEM((7, count, width), BF16),
                pltpu.VMEM((8, 8, 128), F32),
                pltpu.VMEM((8, CAP, 128), BF16),
                pltpu.VMEM((2, slots, width), BF16),
                pltpu.VMEM((slots, width), BF16),
                pltpu.VMEM((slots, 3 * HID), BF16),
                pltpu.VMEM((8, count, width), BF16),
                pltpu.VMEM((8, count, width), BF16),
                pltpu.VMEM((4, count, width), BF16),
                pltpu.VMEM((4, count, width), BF16),
                pltpu.VMEM((4, count, width), BF16),
                pltpu.VMEM((4, count, width), BF16),
                pltpu.VMEM((6, count, width), BF16),
                pltpu.VMEM((8, 8, 128), F32),
                pltpu.VMEM((8, 8, 128), F32),
                pltpu.VMEM((nz, NY, 16, width), F32),
                pltpu.VMEM((chains_a, hr_a, nz, 16, WIDE), BF16),
                pltpu.VMEM((chains_a, hr_a, nz, 16, WIDE), BF16),
                pltpu.VMEM((chains_a, hl_a, nz, 16, WIDE), BF16),
                pltpu.VMEM((chains_a, hl_a, nz, 16, WIDE), BF16),
                pltpu.VMEM((chains_b, hr_b, NY, 16, WIDE), BF16),
                pltpu.VMEM((chains_b, hr_b, NY, 16, WIDE), BF16),
                pltpu.VMEM((chains_b, hl_b, NY, 16, WIDE), BF16),
                pltpu.VMEM((chains_b, hl_b, NY, 16, WIDE), BF16),
                pltpu.VMEM((nz, 16, COLS_A), F32),
                pltpu.VMEM((NY, 16, width - COLS_A), F32),
                pltpu.VMEM((nz, 16, COLS_A), BF16),
                pltpu.VMEM((NY, 16, width - COLS_A), BF16),
                pltpu.VMEM((nz - 1, 16, COLS_A), BF16),
                pltpu.VMEM((NY - 1, 16, width - COLS_A), BF16),
                pltpu.SemaphoreType.DMA((5,)),
                pltpu.SemaphoreType.DMA((count_messages,)),
                pltpu.SemaphoreType.DMA((count_messages,)),
            ],
            compiler_params=pltpu.CompilerParams(
                collective_id=0, has_side_effects=True, vmem_limit_bytes=62 * 1024 * 1024
            ),
        )(
            tokens,
            cotangent,
            expert_ids.T,
            route_weights.T,
            expert_weights.reshape(expert_weights.shape[1:]),
        )
        outs = (lat, tg, rg, eg)
        lat, tg, rg, eg = pl.pallas_call(
            pass_on,
            out_shape=tuple(jax.ShapeDtypeStruct(o.shape, o.dtype) for o in outs),
            in_specs=[vmem] * 4,
            out_specs=(vmem,) * 4,
            compiler_params=pltpu.CompilerParams(vmem_limit_bytes=62 * 1024 * 1024),
        )(*outs)
        return lat, tg, rg.T, eg[None]

    return jax.shard_map(
        body,
        mesh=mesh,
        in_specs=(
            P(("dp", "expert"), None),
            P(("dp", "expert"), None),
            P(("dp", "expert"), None),
            P(("dp", "expert"), None),
            P("expert", None, None),
        ),
        out_specs=(
            P(("dp", "expert"), None),
            P(("dp", "expert"), None),
            P(("dp", "expert"), None),
            P("expert", "dp", None),
        ),
        check_vma=False,
    )
```

```python
import math

import jax
import jax.numpy as jnp
from jax import lax
from jax.experimental import pallas as pl
from jax.experimental.pallas import tpu as pltpu
from jax.sharding import PartitionSpec as P

MESH = pl.DeviceIdType.MESH
F32 = jnp.float32
BF16 = jnp.bfloat16

HID = 512
CAP = 64
NX = 4
NY = 8
ROWS = 512
WIDE = 128
PARTS_A = 2
PARTS_B = 2
CHAINS_A = 4
COLS_A = CHAINS_A * WIDE

NT = (((1,), (1,)), ((), ()))
TN = (((0,), (0,)), ((), ()))


def dot(a, b, dims=(((1,), (0,)), ((), ()))):
    return lax.dot_general(a, b, dims, preferred_element_type=F32)


class Messages:
    def __init__(self, send_sems, recv_sems):
        self.send_sems, self.recv_sems, self.index = send_sems, recv_sems, {}

    def make(self, key, src, dst, device):
        i = self.index.setdefault(key, len(self.index))
        return pltpu.make_async_remote_copy(
            src_ref=src,
            dst_ref=dst,
            send_sem=self.send_sems.at[i],
            recv_sem=self.recv_sems.at[i],
            device_id=device,
            device_id_type=MESH,
        )

    def start(self, key, src, dst, device):
        copy = self.make(key, src, dst, device)
        copy.start()
        return copy


class Chain:
    def __init__(self, net, key, pos, n, sign, along, term, bufs):
        self.net, self.pos, self.n, self.term = net, pos, n, term
        far, near = n // 2, n - 1 - n // 2
        send_f, recv_f, send_n, recv_n = bufs
        self.ways = (
            (key + ("far",), sign, far, along(sign), send_f, recv_f),
            (key + ("near",), -sign, near, along(-sign), send_n, recv_n),
        )

    def copy(self, way, s):
        key, _, _, device, send, recv = way
        return self.net.make(key + (s,), send.at[s], recv.at[s], device)

    def step(self, s):
        for way in self.ways:
            _, sign, hops, _, send, recv = way
            if s >= hops:
                continue
            values = self.term(lax.rem(self.pos + self.n + sign * (hops - s), self.n))
            if s:
                self.copy(way, s - 1).wait_recv()
            for e in range(2):
                v = values[e]
                if s:
                    v = v + recv[s - 1, e].astype(F32)
                send[s, e] = v.astype(BF16)
            self.copy(way, s).start()

    def final(self):
        values = self.term(self.pos)
        for way in self.ways:
            hops, recv = way[2], way[5]
            self.copy(way, hops - 1).wait_recv()
            values = [v + recv[hops - 1, e].astype(F32) for e, v in enumerate(values)]
        return values

    def sent(self):
        return [self.copy(way, s) for way in self.ways for s in range(way[2])]


def kernel(
    nz, factor,
    tok_h, cot_h, ids_h, wts_h, ew,
    lat_o, tg_o, rg_o, eg_o,
    tok, cot, ids, wts, weights, tok_b, cot_b, route_b, pick_b, rhs_b, cot_s, grad_s,
    con_l, con_g, sib_l, sib_g, part_l, part_g, xin, rg_s, rg_r,
    term_b, term_c, sib_b, eg_s, eg_r, asr, arr, asl, arl, bsr, brr, bsl, brl, sum_a, sum_b, two_a, two_b, in_a, in_b,
    local_sems, send_sems, recv_sems,
):
    dp, ex = lax.axis_index("dp"), lax.axis_index("expert")
    z, y = lax.div(dp, NY), lax.rem(dp, NY)
    x, c = lax.div(ex, 2), lax.rem(ex, 2)

    def in_group(dx, dc):
        return {"dp": dp, "expert": lax.rem(x + dx + NX, NX) * 2 + lax.rem(c + dc, 2)}

    def along_y(d):
        return {"dp": z * NY + lax.rem(y + d + NY, NY), "expert": ex}

    def along_z(d):
        return {"dp": lax.rem(z + d + nz, nz) * NY + y, "expert": ex}

    offset = (0, -1, 1, 2)
    inverse = (0, 2, 1, 3)

    loads = [
        pltpu.make_async_copy(src, dst, local_sems.at[i])
        for i, (src, dst) in enumerate(
            ((ids_h, ids), (wts_h, wts), (tok_h, tok), (cot_h, cot), (ew, weights))
        )
    ]
    for load in loads:
        load.start()
    barrier = pltpu.get_barrier_semaphore()
    def farthest_first(n):
        return sorted(range(1, n), key=lambda d: -min(d, n - d))

    group = [in_group(offset[k % 4], k // 4) for k in range(1, 8)]
    partners_0 = [along_z(d) for d in farthest_first(nz)] + [along_y(1), along_y(-1)] + group
    partners_1 = [along_y(d) for d in farthest_first(NY)] + [along_z(1), along_z(-1)] + group

    def greet(partners):
        for device in partners:
            pl.semaphore_signal(barrier, inc=1, device_id=device, device_id_type=MESH)

    pl.when(c == 0)(lambda: greet(partners_0))
    pl.when(c == 1)(lambda: greet(partners_1))
    for load in loads[:2]:
        load.wait()
    expert_of = lax.broadcasted_iota(jnp.int32, (8, 128), 0)
    w_in = wts[...].astype(F32)
    id_in = ids[...]
    route_b[0] = sum(
        jnp.where(id_in[k : k + 1] == expert_of, w_in[k : k + 1], 0.0) for k in range(2)
    )
    for load in loads[2:4]:
        load.wait()
    pl.semaphore_wait(barrier, jnp.where(c == 0, len(partners_0), len(partners_1)))

    net = Messages(send_sems, recv_sems)
    right, left, sibling = in_group(1, 0), in_group(-1, 0), in_group(0, 1)

    route_in = [
        net.start(("route", k), route_b.at[0], route_b.at[inverse[k % 4] + k // 4 * 4], in_group(offset[k % 4], k // 4))
        for k in range(1, 8)
    ]
    sib_t, sib_c = [None] * 4, [None] * 4
    tok_l = net.start(("c", 1), tok, tok_b.at[0], right)
    cot_r = net.start(("c", 2), cot, cot_b.at[1], left)
    sib_t[0] = net.start(("c", 3), tok, tok_b.at[3], sibling)
    sib_c[0] = net.start(("c", 4), cot, cot_b.at[3], sibling)

    def block(k):
        return (tok, cot) if k == 0 else (tok_b.at[k - 1], cot_b.at[k - 1])

    for m in route_in:
        m.wait_recv()
    rows = jnp.concatenate([route_b[k, pl.ds(ex, 1), :] for k in range(8)], axis=0)
    before = (
        lax.broadcasted_iota(jnp.int32, (128, 128), 0) < lax.broadcasted_iota(jnp.int32, (128, 128), 1)
    ).astype(F32)
    ranks = dot(jnp.where(rows > 0, 1.0, 0.0).astype(BF16), before.astype(BF16))
    seat = lax.broadcasted_iota(jnp.int32, (CAP, 128), 0).astype(F32)
    loads[4].wait()

    def stage(slots, base):
        size = CAP * len(slots)
        own = pl.ds(base, size)
        w_of = []
        for i, k in enumerate(slots):
            at = pl.ds(base + CAP * i, CAP)
            pick = jnp.where((ranks[k : k + 1] == seat) & (rows[k : k + 1] > 0), 1.0, 0.0)
            w = jnp.sum(pick * rows[k : k + 1], axis=1, keepdims=True)
            w_of.append(w)
            pick = pick.astype(BF16)
            pick_b[k] = pick
            t_ref, c_ref = block(k)
            rhs_b[0, at, :] = dot(pick, t_ref[...]).astype(BF16)
            cots = dot(pick, c_ref[...])
            cot_s[at, :] = cots.astype(BF16)
            rhs_b[1, at, :] = (w * cots).astype(BF16)
        w = jnp.concatenate(w_of, axis=0)
        both = dot(rhs_b[0, own, :], weights[: 2 * HID, :], NT)
        gate, up = both[:, :HID], both[:, HID:]
        sig = 1.0 / (1.0 + jnp.exp(-gate))
        act = gate * sig
        hidden = (act * up).astype(BF16)
        grad_s[own, 2 * HID :] = hidden
        d_hidden = dot(rhs_b[1, own, :], weights[2 * HID :, :], NT)
        grad_s[own, HID : 2 * HID] = (d_hidden * act).astype(BF16)
        grad_s[own, :HID] = (d_hidden * up * sig * (1.0 + gate * (1.0 - sig))).astype(BF16)
        out = dot(hidden, weights[2 * HID :, :]).astype(BF16).astype(F32)
        r_grad = jnp.sum(cot_s[own, :].astype(F32) * out, axis=1, keepdims=True)
        out = (w * out).astype(BF16)
        d_x = dot(grad_s[own, : 2 * HID], weights[: 2 * HID, :]).astype(BF16)
        for i, k in enumerate(slots):
            pick = pick_b[k]
            part = slice(CAP * i, CAP * (i + 1))
            con_l[k] = dot(pick, out[part], TN).astype(BF16)
            con_g[k] = dot(pick, d_x[part], TN).astype(BF16)
            line = jnp.sum(pick.astype(F32) * r_grad[part], axis=0, keepdims=True)
            rg_s[k] = jnp.broadcast_to(line, (8, 128))

    sib_out = {}

    def to_sibling(k):
        sib_out[k] = (
            net.start(("sib_l", k), con_l.at[k + 4], sib_l.at[k], sibling),
            net.start(("sib_g", k), con_g.at[k + 4], sib_g.at[k], sibling),
        )

    def chip_part(k):
        for m in sib_out[k]:
            m.wait_recv()
        part_l[k] = (con_l[k].astype(F32) + sib_l[k].astype(F32)).astype(BF16)
        part_g[k] = (con_g[k].astype(F32) + sib_g[k].astype(F32)).astype(BF16)

    sib_t[0].wait_recv()
    sib_c[0].wait_recv()
    stage((0, 4), 0)
    cot_l = net.start(("c", 5), cot, cot_b.at[0], right)
    tok_r = net.start(("c", 6), tok, tok_b.at[1], left)
    to_sibling(0)

    tok_l.wait_recv()
    opp_t = net.start(("c", 7), tok_b.at[0], tok_b.at[2], right)
    sib_t[1] = net.start(("c", 8), tok_b.at[0], tok_b.at[4], sibling)
    cot_r.wait_recv()
    opp_c = net.start(("c", 9), cot_b.at[1], cot_b.at[2], left)
    sib_c[2] = net.start(("c", 10), cot_b.at[1], cot_b.at[5], sibling)
    cot_l.wait_recv()
    sib_c[1] = net.start(("c", 11), cot_b.at[0], cot_b.at[4], sibling)
    tok_r.wait_recv()
    sib_t[2] = net.start(("c", 12), tok_b.at[1], tok_b.at[5], sibling)
    for k in (1, 2):
        sib_t[k].wait_recv()
        sib_c[k].wait_recv()
    stage((1, 2, 5, 6), 2 * CAP)
    to_sibling(1)
    to_sibling(2)
    opp_t.wait_recv()
    sib_t[3] = net.start(("c", 13), tok_b.at[2], tok_b.at[6], sibling)
    opp_c.wait_recv()
    sib_c[3] = net.start(("c", 14), cot_b.at[2], cot_b.at[6], sibling)
    chip_part(1)
    chip_part(2)
    near_g = net.start(("c", 15), part_g.at[2], xin.at[0], right)
    near_l = net.start(("c", 16), part_l.at[1], xin.at[1], left)

    sib_t[3].wait_recv()
    sib_c[3].wait_recv()
    stage((3, 7), 6 * CAP)
    to_sibling(3)

    early = [*route_in, tok_l, cot_l, tok_r, cot_r, *sib_t, *sib_c, opp_t, opp_c, near_g, near_l]
    early += [m for pair in sib_out.values() for m in pair]

    half = nz // 2
    wide = term_b.shape[-1]
    chains_b = wide // WIDE - CHAINS_A

    def rows_of(low, high):
        def some_rows(i, carry):
            at = pl.multiple_of(i * ROWS, ROWS)
            v = dot(grad_s[:, pl.ds(at, ROWS)], rhs_b[lax.div(at, 2 * HID), :, low:high], TN)
            v = v.reshape(ROWS // 128, NY, 16, high - low)
            own = pl.ds(i * (ROWS // 128), ROWS // 128)
            term_b[own, :, :, low:high] = v
            term_c[own, :, :, low:high] = v.astype(BF16)
            return carry

        lax.fori_loop(0, 3 * HID // ROWS, some_rows, 0)

    def order(i):
        d = 0 if i == nz - 1 else half - (i + 1) // 2 if i % 2 else half + i // 2
        return lax.rem(z + d, nz)

    def term_of_b(i):
        t = order(i)
        part = (t, slice(None), slice(None), slice(COLS_A, wide))
        return net.make(("term_b", i), term_c.at[part], sib_b.at[part], sibling)

    def term_of_a(q):
        part = (slice(None), slice(None), slice(None), slice(q * WIDE, (q + 1) * WIDE))
        return net.make(("term_a", q), term_c.at[part], sib_b.at[part], sibling)

    def chain_a(q):
        cols = slice(q * WIDE, (q + 1) * WIDE)

        def term(t):
            return [term_b[:, t, :, cols], sib_b[:, t, :, cols].astype(F32)]

        bufs = [b.at[q] for b in (asr, arr, asl, arl)]
        return Chain(net, ("A", q), y, NY, 1 - q % 2 * 2, along_y, term, bufs)

    def chain_b(q):
        cols = slice(COLS_A + q * WIDE, COLS_A + (q + 1) * WIDE)

        def term(t):
            return [sib_b[t, :, :, cols].astype(F32), term_b[t, :, :, cols]]

        bufs = [b.at[q] for b in (bsr, brr, bsl, brl)]
        return Chain(net, ("B", q), z, nz, 1 - q % 2 * 2, along_z, term, bufs)

    all_a = [chain_a(q) for q in range(CHAINS_A)]
    all_b = [chain_b(q) for q in range(chains_b)]

    rows_of(0, wide)

    def send_a():
        for q in range(CHAINS_A):
            term_of_a(q).start()

    pl.when(c == 1)(send_a)
    def send_b():
        for i in range(nz):
            term_of_b(i).start()

    pl.when(c == 0)(send_b)

    def far_l():
        return net.make("far_l", part_l.at[3], xin.at[2], right)

    def far_g():
        return net.make("far_g", part_g.at[3], xin.at[3], left)

    def last_l():
        return net.make("last_l", part_l.at[2], xin.at[4], right)

    def last_g():
        return net.make("last_g", part_g.at[1], xin.at[5], left)

    def route_out(k):
        to = inverse[k % 4] + k // 4 * 4
        return net.make(("rg", k), rg_s.at[k], rg_r.at[to], in_group(offset[k % 4], k // 4))

    def far_parts():
        chip_part(3)
        far_l().start()
        far_g().start()
        for k in range(1, 8):
            route_out(k).start()

    def last_parts():
        far_l().wait_recv()
        part_l[2] = (part_l[2].astype(F32) + xin[2].astype(F32)).astype(BF16)
        last_l().start()
        far_g().wait_recv()
        part_g[1] = (part_g[1].astype(F32) + xin[3].astype(F32)).astype(BF16)
        last_g().start()
        chip_part(0)

    def outputs():
        near_g.wait_recv()
        last_g().wait_recv()
        tg_o[...] = (part_g[0].astype(F32) + xin[0].astype(F32) + xin[5].astype(F32)).astype(BF16)
        near_l.wait_recv()
        last_l().wait_recv()
        lat_o[...] = (part_l[0].astype(F32) + xin[1].astype(F32) + xin[4].astype(F32)).astype(BF16)
        route = [jnp.zeros((1, 128), F32), jnp.zeros((1, 128), F32)]
        for k in range(1, 8):
            route_out(k).wait_recv()
        for k in range(8):
            line = rg_s[0, 0:1, :] if k == 0 else rg_r[k, 0:1, :]
            expert = in_group(offset[k % 4], k // 4)["expert"]
            for j in range(2):
                route[j] = route[j] + jnp.where(id_in[j : j + 1] == expert, line, 0.0)
        rg_o[...] = jnp.concatenate(route, axis=0)
        for m in (far_l(), far_g(), last_l(), last_g(), *(route_out(k) for k in range(1, 8))):
            m.wait_send()

    def share(low, high):
        part = (slice(None), slice(low, high))
        return net.make(("share", low), eg_s.at[part], eg_r.at[part], sibling)

    def run(events):
        for _, event in sorted(events, key=lambda e: e[0]):
            event()

    def finish(own, summed, place, incoming, arrived, low, high):
        outputs()
        for m in incoming:
            m.wait_recv()
        for e in (1 - own, own):
            total = factor * (summed[place, e] + jnp.sum(arrived[:, e].astype(F32), axis=0))
            if e == own:
                eg_o[:, low:high] = total
            else:
                eg_s[:, low:high] = total
                to_other = share(low, high)
                to_other.start()
        other = (COLS_A, wide) if low == 0 else (0, COLS_A)
        for m in incoming:
            m.wait_send()
        share(*other).wait_recv()
        eg_o[:, other[0] : other[1]] = eg_r[:, other[0] : other[1]]
        to_other.wait_send()

    def core_0():
        a_in = []

        def first(q):
            term_of_a(q).wait_recv()
            all_a[q].step(0)

        def final(q):
            cols = slice(q * WIDE, (q + 1) * WIDE)
            for e, v in enumerate(all_a[q].final()):
                sum_a[:, e, :, cols] = v
                two_a[:, e, :, cols] = v.astype(BF16)

        def second(i):
            cols = slice(i * COLS_A // PARTS_A, (i + 1) * COLS_A // PARTS_A)
            a_in.extend(
                net.start(("a", i, d), two_a.at[lax.rem(z + d, nz), :, :, cols], in_a.at[d - 1, :, :, cols], along_z(d))
                for d in farthest_first(nz)
            )

        events = [(0.99, far_parts), (2.3, last_parts)]
        for q in range(CHAINS_A):
            events.append((q / CHAINS_A, lambda q=q: first(q)))
            for s in range(1, NY // 2):
                events.append((s + q / CHAINS_A, lambda q=q, s=s: all_a[q].step(s)))
            events.append((NY // 2 + q / CHAINS_A, lambda q=q: final(q)))
        for i in range(PARTS_A):
            last = (i + 1) * CHAINS_A // PARTS_A - 1
            events.append((NY // 2 + last / CHAINS_A + 0.01, lambda i=i: second(i)))
        run(events)
        finish(0, sum_a, z, a_in, in_a, 0, COLS_A)
        for m in [term_of_b(i) for i in range(nz)] + [m for chain in all_a for m in chain.sent()]:
            m.wait_send()

    def core_1():
        b_in = []

        def step(q, s):
            if q == 0:
                for i in (2 * s + 1, 2 * s + 2) if s else (0, 1, 2):
                    if i < nz:
                        term_of_b(i).wait_recv()
            all_b[q].step(s)

        def final(q):
            cols = slice(q * WIDE, (q + 1) * WIDE)
            for e, v in enumerate(all_b[q].final()):
                sum_b[:, e, :, cols] = v
                two_b[:, e, :, cols] = v.astype(BF16)

        def second(i):
            cols = slice(i * (wide - COLS_A) // PARTS_B, (i + 1) * (wide - COLS_A) // PARTS_B)
            b_in.extend(
                net.start(("b", i, d), two_b.at[lax.rem(y + d, NY), :, :, cols], in_b.at[d - 1, :, :, cols], along_y(d))
                for d in farthest_first(NY)
            )

        events = [(0.99, far_parts), (3.3, last_parts)]
        for q in range(chains_b):
            for s in range(half):
                events.append((s + q / chains_b, lambda q=q, s=s: step(q, s)))
            events.append((half + q / chains_b, lambda q=q: final(q)))
        for i in range(PARTS_B):
            last = (i + 1) * chains_b // PARTS_B - 1
            events.append((half + last / chains_b + 0.01, lambda i=i: second(i)))
        run(events)
        finish(1, sum_b, y, b_in, in_b, COLS_A, wide)
        for m in [term_of_a(q) for q in range(CHAINS_A)] + [m for chain in all_b for m in chain.sent()]:
            m.wait_send()

    pl.when(c == 0)(core_0)
    pl.when(c == 1)(core_1)
    for m in early:
        m.wait_send()


def pass_on(*refs):
    for i in range(4):
        refs[4 + i][...] = refs[i][...]


def solution(mesh):
    n_dp, n_ex = mesh.shape["dp"], mesh.shape["expert"]
    nz = n_dp // NY

    def body(tokens, cotangent, expert_ids, route_weights, expert_weights):
        count, width = tokens.shape
        slots = CAP * n_ex
        factor = 1.0 / math.sqrt(count * n_dp * n_ex)
        chains_a, chains_b = CHAINS_A, width // WIDE - CHAINS_A
        hr_a, hl_a = NY // 2, NY - 1 - NY // 2
        hr_b, hl_b = nz // 2, nz - 1 - nz // 2
        vmem = pl.BlockSpec(memory_space=pltpu.VMEM)
        count_messages = 7 + 6 + 6 + 2 + 8 + 6 + 7 + 2 + nz + chains_a + chains_a * (NY - 1) + chains_b * (nz - 1) + PARTS_A * (nz - 1) + PARTS_B * (NY - 1)
        lat, tg, rg, eg = pl.pallas_call(
            lambda *refs: kernel(nz, factor, *refs),
            out_shape=(
                jax.ShapeDtypeStruct((count, width), BF16),
                jax.ShapeDtypeStruct((count, width), BF16),
                jax.ShapeDtypeStruct((2, count), F32),
                jax.ShapeDtypeStruct((16, width), F32),
            ),
            in_specs=[pl.BlockSpec(memory_space=pltpu.HBM)] * 5,
            out_specs=(vmem,) * 4,
            scratch_shapes=[
                pltpu.VMEM((count, width), BF16),
                pltpu.VMEM((count, width), BF16),
                pltpu.VMEM((2, count), jnp.int32),
                pltpu.VMEM((2, count), BF16),
                pltpu.VMEM((3 * HID, width), BF16),
                pltpu.VMEM((7, count, width), BF16),
                pltpu.VMEM((7, count, width), BF16),
                pltpu.VMEM((8, 8, 128), F32),
                pltpu.VMEM((8, CAP, 128), BF16),
                pltpu.VMEM((2, slots, width), BF16),
                pltpu.VMEM((slots, width), BF16),
                pltpu.VMEM((slots, 3 * HID), BF16),
                pltpu.VMEM((8, count, width), BF16),
                pltpu.VMEM((8, count, width), BF16),
                pltpu.VMEM((4, count, width), BF16),
                pltpu.VMEM((4, count, width), BF16),
                pltpu.VMEM((4, count, width), BF16),
                pltpu.VMEM((4, count, width), BF16),
                pltpu.VMEM((6, count, width), BF16),
                pltpu.VMEM((8, 8, 128), F32),
                pltpu.VMEM((8, 8, 128), F32),
                pltpu.VMEM((nz, NY, 16, width), F32),
                pltpu.VMEM((nz, NY, 16, width), BF16),
                pltpu.VMEM((nz, NY, 16, width), BF16),
                pltpu.VMEM((16, width), F32),
                pltpu.VMEM((16, width), F32),
                pltpu.VMEM((chains_a, hr_a, 2, nz, 16, WIDE), BF16),
                pltpu.VMEM((chains_a, hr_a, 2, nz, 16, WIDE), BF16),
                pltpu.VMEM((chains_a, hl_a, 2, nz, 16, WIDE), BF16),
                pltpu.VMEM((chains_a, hl_a, 2, nz, 16, WIDE), BF16),
                pltpu.VMEM((chains_b, hr_b, 2, NY, 16, WIDE), BF16),
                pltpu.VMEM((chains_b, hr_b, 2, NY, 16, WIDE), BF16),
                pltpu.VMEM((chains_b, hl_b, 2, NY, 16, WIDE), BF16),
                pltpu.VMEM((chains_b, hl_b, 2, NY, 16, WIDE), BF16),
                pltpu.VMEM((nz, 2, 16, COLS_A), F32),
                pltpu.VMEM((NY, 2, 16, width - COLS_A), F32),
                pltpu.VMEM((nz, 2, 16, COLS_A), BF16),
                pltpu.VMEM((NY, 2, 16, width - COLS_A), BF16),
                pltpu.VMEM((nz - 1, 2, 16, COLS_A), BF16),
                pltpu.VMEM((NY - 1, 2, 16, width - COLS_A), BF16),
                pltpu.SemaphoreType.DMA((5,)),
                pltpu.SemaphoreType.DMA((count_messages,)),
                pltpu.SemaphoreType.DMA((count_messages,)),
            ],
            compiler_params=pltpu.CompilerParams(
                collective_id=0, has_side_effects=True, vmem_limit_bytes=62 * 1024 * 1024
            ),
        )(
            tokens,
            cotangent,
            expert_ids.T,
            route_weights.T,
            expert_weights.reshape(expert_weights.shape[1:]),
        )
        outs = (lat, tg, rg, eg)
        lat, tg, rg, eg = pl.pallas_call(
            pass_on,
            out_shape=tuple(jax.ShapeDtypeStruct(o.shape, o.dtype) for o in outs),
            in_specs=[vmem] * 4,
            out_specs=(vmem,) * 4,
            compiler_params=pltpu.CompilerParams(vmem_limit_bytes=62 * 1024 * 1024),
        )(*outs)
        return lat, tg, rg.T, eg[None]

    return jax.shard_map(
        body,
        mesh=mesh,
        in_specs=(
            P(("dp", "expert"), None),
            P(("dp", "expert"), None),
            P(("dp", "expert"), None),
            P(("dp", "expert"), None),
            P("expert", None, None),
        ),
        out_specs=(
            P(("dp", "expert"), None),
            P(("dp", "expert"), None),
            P(("dp", "expert"), None),
            P("expert", "dp", None),
        ),
        check_vma=False,
    )
```

```python
import math

import jax
import jax.numpy as jnp
from jax import lax
from jax.experimental import pallas as pl
from jax.experimental.pallas import tpu as pltpu
from jax.sharding import PartitionSpec as P

MESH = pl.DeviceIdType.MESH
F32 = jnp.float32
BF16 = jnp.bfloat16

HID = 512
CAP = 64
NX = 4
NY = 8
ROWS = 512
WIDE = 128
PARTS_A = 2
PARTS_B = 2
CHAINS_A = 4
COLS_A = CHAINS_A * WIDE

NT = (((1,), (1,)), ((), ()))
TN = (((0,), (0,)), ((), ()))


def dot(a, b, dims=(((1,), (0,)), ((), ()))):
    return lax.dot_general(a, b, dims, preferred_element_type=F32)


class Messages:
    def __init__(self, send_sems, recv_sems):
        self.send_sems, self.recv_sems, self.index = send_sems, recv_sems, {}

    def make(self, key, src, dst, device):
        i = self.index.setdefault(key, len(self.index))
        return pltpu.make_async_remote_copy(
            src_ref=src,
            dst_ref=dst,
            send_sem=self.send_sems.at[i],
            recv_sem=self.recv_sems.at[i],
            device_id=device,
            device_id_type=MESH,
        )

    def start(self, key, src, dst, device):
        copy = self.make(key, src, dst, device)
        copy.start()
        return copy


class Chain:
    def __init__(self, net, key, pos, n, sign, along, term, bufs):
        self.net, self.pos, self.n, self.term = net, pos, n, term
        far, near = n // 2, n - 1 - n // 2
        send_f, recv_f, send_n, recv_n = bufs
        self.ways = (
            (key + ("far",), sign, far, along(sign), send_f, recv_f),
            (key + ("near",), -sign, near, along(-sign), send_n, recv_n),
        )

    def copy(self, way, s):
        key, _, _, device, send, recv = way
        return self.net.make(key + (s,), send.at[s], recv.at[s], device)

    def step(self, s):
        for way in self.ways:
            _, sign, hops, _, send, recv = way
            if s >= hops:
                continue
            values = self.term(lax.rem(self.pos + self.n + sign * (hops - s), self.n))
            if s:
                self.copy(way, s - 1).wait_recv()
            for e in range(2):
                v = values[e]
                if s:
                    v = v + recv[s - 1, e].astype(F32)
                send[s, e] = v.astype(BF16)
            self.copy(way, s).start()

    def final(self):
        values = self.term(self.pos)
        for way in self.ways:
            hops, recv = way[2], way[5]
            self.copy(way, hops - 1).wait_recv()
            values = [v + recv[hops - 1, e].astype(F32) for e, v in enumerate(values)]
        return values

    def sent(self):
        return [self.copy(way, s) for way in self.ways for s in range(way[2])]


def kernel(
    nz, factor,
    tok_h, cot_h, ids_h, wts_h, ew,
    lat_o, tg_o, rg_o, eg_o,
    tok, cot, ids, wts, weights, tok_b, cot_b, route_b, pick_b, rhs_b, cot_s, grad_s,
    con_l, con_g, sib_l, sib_g, part_l, part_g, xin, rg_s, rg_r,
    term_b, term_c, sib_b, eg_s, eg_r, asr, arr, asl, arl, bsr, brr, bsl, brl, sum_a, sum_b, two_a, two_b, in_a, in_b,
    local_sems, send_sems, recv_sems,
):
    dp, ex = lax.axis_index("dp"), lax.axis_index("expert")
    z, y = lax.div(dp, NY), lax.rem(dp, NY)
    x, c = lax.div(ex, 2), lax.rem(ex, 2)

    def in_group(dx, dc):
        return {"dp": dp, "expert": lax.rem(x + dx + NX, NX) * 2 + lax.rem(c + dc, 2)}

    def along_y(d):
        return {"dp": z * NY + lax.rem(y + d + NY, NY), "expert": ex}

    def along_z(d):
        return {"dp": lax.rem(z + d + nz, nz) * NY + y, "expert": ex}

    offset = (0, -1, 1, 2)
    inverse = (0, 2, 1, 3)

    loads = [
        pltpu.make_async_copy(src, dst, local_sems.at[i])
        for i, (src, dst) in enumerate(
            ((ids_h, ids), (wts_h, wts), (tok_h, tok), (cot_h, cot), (ew, weights))
        )
    ]
    for load in loads:
        load.start()
    barrier = pltpu.get_barrier_semaphore()
    def farthest_first(n):
        return sorted(range(1, n), key=lambda d: -min(d, n - d))

    group = [in_group(offset[k % 4], k // 4) for k in range(1, 8)]
    partners_0 = [along_z(d) for d in farthest_first(nz)] + [along_y(1), along_y(-1)] + group
    partners_1 = [along_y(d) for d in farthest_first(NY)] + [along_z(1), along_z(-1)] + group

    def greet(partners):
        for device in partners:
            pl.semaphore_signal(barrier, inc=1, device_id=device, device_id_type=MESH)

    pl.when(c == 0)(lambda: greet(partners_0))
    pl.when(c == 1)(lambda: greet(partners_1))
    for load in loads[:2]:
        load.wait()
    expert_of = lax.broadcasted_iota(jnp.int32, (8, 128), 0)
    w_in = wts[...].astype(F32)
    id_in = ids[...]
    route_b[0] = sum(
        jnp.where(id_in[k : k + 1] == expert_of, w_in[k : k + 1], 0.0) for k in range(2)
    )
    for load in loads[2:4]:
        load.wait()
    pl.semaphore_wait(barrier, jnp.where(c == 0, len(partners_0), len(partners_1)))

    net = Messages(send_sems, recv_sems)
    right, left, sibling = in_group(1, 0), in_group(-1, 0), in_group(0, 1)

    sib_t, sib_c = [None] * 4, [None] * 4
    tok_l = net.start(("c", 1), tok, tok_b.at[0], right)
    cot_r = net.start(("c", 2), cot, cot_b.at[1], left)
    sib_t[0] = net.start(("c", 3), tok, tok_b.at[3], sibling)
    sib_c[0] = net.start(("c", 4), cot, cot_b.at[3], sibling)
    route_in = [
        net.start(("route", k), route_b.at[0], route_b.at[inverse[k % 4] + k // 4 * 4], in_group(offset[k % 4], k // 4))
        for k in range(1, 8)
    ]

    def block(k):
        return (tok, cot) if k == 0 else (tok_b.at[k - 1], cot_b.at[k - 1])

    for m in route_in:
        m.wait_recv()
    rows = jnp.concatenate([route_b[k, pl.ds(ex, 1), :] for k in range(8)], axis=0)
    before = (
        lax.broadcasted_iota(jnp.int32, (128, 128), 0) < lax.broadcasted_iota(jnp.int32, (128, 128), 1)
    ).astype(F32)
    ranks = dot(jnp.where(rows > 0, 1.0, 0.0).astype(BF16), before.astype(BF16))
    seat = lax.broadcasted_iota(jnp.int32, (CAP, 128), 0).astype(F32)
    loads[4].wait()

    def stage(slots, base):
        size = CAP * len(slots)
        own = pl.ds(base, size)
        w_of = []
        for i, k in enumerate(slots):
            at = pl.ds(base + CAP * i, CAP)
            pick = jnp.where((ranks[k : k + 1] == seat) & (rows[k : k + 1] > 0), 1.0, 0.0)
            w = jnp.sum(pick * rows[k : k + 1], axis=1, keepdims=True)
            w_of.append(w)
            pick = pick.astype(BF16)
            pick_b[k] = pick
            t_ref, c_ref = block(k)
            rhs_b[0, at, :] = dot(pick, t_ref[...]).astype(BF16)
            cots = dot(pick, c_ref[...])
            cot_s[at, :] = cots.astype(BF16)
            rhs_b[1, at, :] = (w * cots).astype(BF16)
        w = jnp.concatenate(w_of, axis=0)
        both = dot(rhs_b[0, own, :], weights[: 2 * HID, :], NT)
        gate, up = both[:, :HID], both[:, HID:]
        sig = 1.0 / (1.0 + jnp.exp(-gate))
        act = gate * sig
        hidden = (act * up).astype(BF16)
        grad_s[own, 2 * HID :] = hidden
        d_hidden = dot(rhs_b[1, own, :], weights[2 * HID :, :], NT)
        grad_s[own, HID : 2 * HID] = (d_hidden * act).astype(BF16)
        grad_s[own, :HID] = (d_hidden * up * sig * (1.0 + gate * (1.0 - sig))).astype(BF16)
        out = dot(hidden, weights[2 * HID :, :]).astype(BF16).astype(F32)
        r_grad = jnp.sum(cot_s[own, :].astype(F32) * out, axis=1, keepdims=True)
        out = (w * out).astype(BF16)
        d_x = dot(grad_s[own, : 2 * HID], weights[: 2 * HID, :]).astype(BF16)
        for i, k in enumerate(slots):
            pick = pick_b[k]
            part = slice(CAP * i, CAP * (i + 1))
            con_l[k] = dot(pick, out[part], TN).astype(BF16)
            con_g[k] = dot(pick, d_x[part], TN).astype(BF16)
            line = jnp.sum(pick.astype(F32) * r_grad[part], axis=0, keepdims=True)
            rg_s[k] = jnp.broadcast_to(line, (8, 128))

    sib_out = {}

    def to_sibling(k):
        sib_out[k] = (
            net.start(("sib_l", k), con_l.at[k + 4], sib_l.at[k], sibling),
            net.start(("sib_g", k), con_g.at[k + 4], sib_g.at[k], sibling),
        )

    def chip_part(k):
        for m in sib_out[k]:
            m.wait_recv()
        part_l[k] = (con_l[k].astype(F32) + sib_l[k].astype(F32)).astype(BF16)
        part_g[k] = (con_g[k].astype(F32) + sib_g[k].astype(F32)).astype(BF16)

    sib_t[0].wait_recv()
    sib_c[0].wait_recv()
    stage((0, 4), 0)
    cot_l = net.start(("c", 5), cot, cot_b.at[0], right)
    tok_r = net.start(("c", 6), tok, tok_b.at[1], left)
    to_sibling(0)

    tok_l.wait_recv()
    opp_t = net.start(("c", 7), tok_b.at[0], tok_b.at[2], right)
    sib_t[1] = net.start(("c", 8), tok_b.at[0], tok_b.at[4], sibling)
    cot_r.wait_recv()
    opp_c = net.start(("c", 9), cot_b.at[1], cot_b.at[2], left)
    sib_c[2] = net.start(("c", 10), cot_b.at[1], cot_b.at[5], sibling)
    cot_l.wait_recv()
    sib_c[1] = net.start(("c", 11), cot_b.at[0], cot_b.at[4], sibling)
    tok_r.wait_recv()
    sib_t[2] = net.start(("c", 12), tok_b.at[1], tok_b.at[5], sibling)
    for k in (1, 2):
        sib_t[k].wait_recv()
        sib_c[k].wait_recv()
    stage((1, 2, 5, 6), 2 * CAP)
    to_sibling(1)
    to_sibling(2)
    opp_t.wait_recv()
    sib_t[3] = net.start(("c", 13), tok_b.at[2], tok_b.at[6], sibling)
    opp_c.wait_recv()
    sib_c[3] = net.start(("c", 14), cot_b.at[2], cot_b.at[6], sibling)
    chip_part(1)
    chip_part(2)
    near_g = net.start(("c", 15), part_g.at[2], xin.at[0], right)
    near_l = net.start(("c", 16), part_l.at[1], xin.at[1], left)

    sib_t[3].wait_recv()
    sib_c[3].wait_recv()
    stage((3, 7), 6 * CAP)
    to_sibling(3)

    early = [*route_in, tok_l, cot_l, tok_r, cot_r, *sib_t, *sib_c, opp_t, opp_c, near_g, near_l]
    early += [m for pair in sib_out.values() for m in pair]

    half = nz // 2
    wide = term_b.shape[-1]
    chains_b = wide // WIDE - CHAINS_A

    def rows_of(low, high):
        def some_rows(i, carry):
            at = pl.multiple_of(i * ROWS, ROWS)
            v = dot(grad_s[:, pl.ds(at, ROWS)], rhs_b[lax.div(at, 2 * HID), :, low:high], TN)
            v = v.reshape(ROWS // 128, NY, 16, high - low)
            own = pl.ds(i * (ROWS // 128), ROWS // 128)
            term_b[own, :, :, low:high] = v
            term_c[own, :, :, low:high] = v.astype(BF16)
            return carry

        lax.fori_loop(0, 3 * HID // ROWS, some_rows, 0)

    def order(i):
        d = 0 if i == nz - 1 else half - (i + 1) // 2 if i % 2 else half + i // 2
        return lax.rem(z + d, nz)

    def term_of_b(i):
        t = order(i)
        part = (t, slice(None), slice(None), slice(COLS_A, wide))
        return net.make(("term_b", i), term_c.at[part], sib_b.at[part], sibling)

    def term_of_a(q):
        part = (slice(None), slice(None), slice(None), slice(q * WIDE, (q + 1) * WIDE))
        return net.make(("term_a", q), term_c.at[part], sib_b.at[part], sibling)

    def chain_a(q):
        cols = slice(q * WIDE, (q + 1) * WIDE)

        def term(t):
            return [term_b[:, t, :, cols], sib_b[:, t, :, cols].astype(F32)]

        bufs = [b.at[q] for b in (asr, arr, asl, arl)]
        return Chain(net, ("A", q), y, NY, 1 - q % 2 * 2, along_y, term, bufs)

    def chain_b(q):
        cols = slice(COLS_A + q * WIDE, COLS_A + (q + 1) * WIDE)

        def term(t):
            return [sib_b[t, :, :, cols].astype(F32), term_b[t, :, :, cols]]

        bufs = [b.at[q] for b in (bsr, brr, bsl, brl)]
        return Chain(net, ("B", q), z, nz, 1 - q % 2 * 2, along_z, term, bufs)

    all_a = [chain_a(q) for q in range(CHAINS_A)]
    all_b = [chain_b(q) for q in range(chains_b)]

    rows_of(0, wide)

    def send_a():
        for q in range(CHAINS_A):
            term_of_a(q).start()

    pl.when(c == 1)(send_a)
    def send_b():
        for i in range(nz):
            term_of_b(i).start()

    pl.when(c == 0)(send_b)

    def far_l():
        return net.make("far_l", part_l.at[3], xin.at[2], right)

    def far_g():
        return net.make("far_g", part_g.at[3], xin.at[3], left)

    def last_l():
        return net.make("last_l", part_l.at[2], xin.at[4], right)

    def last_g():
        return net.make("last_g", part_g.at[1], xin.at[5], left)

    def route_out(k):
        to = inverse[k % 4] + k // 4 * 4
        return net.make(("rg", k), rg_s.at[k], rg_r.at[to], in_group(offset[k % 4], k // 4))

    def far_parts():
        chip_part(3)
        far_l().start()
        far_g().start()
        for k in range(1, 8):
            route_out(k).start()

    def last_parts():
        far_l().wait_recv()
        part_l[2] = (part_l[2].astype(F32) + xin[2].astype(F32)).astype(BF16)
        last_l().start()
        far_g().wait_recv()
        part_g[1] = (part_g[1].astype(F32) + xin[3].astype(F32)).astype(BF16)
        last_g().start()
        chip_part(0)

    def outputs():
        near_g.wait_recv()
        last_g().wait_recv()
        tg_o[...] = (part_g[0].astype(F32) + xin[0].astype(F32) + xin[5].astype(F32)).astype(BF16)
        near_l.wait_recv()
        last_l().wait_recv()
        lat_o[...] = (part_l[0].astype(F32) + xin[1].astype(F32) + xin[4].astype(F32)).astype(BF16)
        route = [jnp.zeros((1, 128), F32), jnp.zeros((1, 128), F32)]
        for k in range(1, 8):
            route_out(k).wait_recv()
        for k in range(8):
            line = rg_s[0, 0:1, :] if k == 0 else rg_r[k, 0:1, :]
            expert = in_group(offset[k % 4], k // 4)["expert"]
            for j in range(2):
                route[j] = route[j] + jnp.where(id_in[j : j + 1] == expert, line, 0.0)
        rg_o[...] = jnp.concatenate(route, axis=0)
        for m in (far_l(), far_g(), last_l(), last_g(), *(route_out(k) for k in range(1, 8))):
            m.wait_send()

    def share(low, high):
        part = (slice(None), slice(low, high))
        return net.make(("share", low), eg_s.at[part], eg_r.at[part], sibling)

    def run(events):
        for _, event in sorted(events, key=lambda e: e[0]):
            event()

    def finish(own, summed, place, incoming, arrived, low, high):
        outputs()
        for m in incoming:
            m.wait_recv()
        for e in (1 - own, own):
            total = factor * (summed[place, e] + jnp.sum(arrived[:, e].astype(F32), axis=0))
            if e == own:
                eg_o[:, low:high] = total
            else:
                eg_s[:, low:high] = total
                to_other = share(low, high)
                to_other.start()
        other = (COLS_A, wide) if low == 0 else (0, COLS_A)
        for m in incoming:
            m.wait_send()
        share(*other).wait_recv()
        eg_o[:, other[0] : other[1]] = eg_r[:, other[0] : other[1]]
        to_other.wait_send()

    def core_0():
        a_in = []

        def first(q):
            term_of_a(q).wait_recv()
            all_a[q].step(0)

        def final(q):
            cols = slice(q * WIDE, (q + 1) * WIDE)
            for e, v in enumerate(all_a[q].final()):
                sum_a[:, e, :, cols] = v
                two_a[:, e, :, cols] = v.astype(BF16)

        def second(i):
            cols = slice(i * COLS_A // PARTS_A, (i + 1) * COLS_A // PARTS_A)
            a_in.extend(
                net.start(("a", i, d), two_a.at[lax.rem(z + d, nz), :, :, cols], in_a.at[d - 1, :, :, cols], along_z(d))
                for d in farthest_first(nz)
            )

        events = [(0.99, far_parts), (2.3, last_parts)]
        for q in range(CHAINS_A):
            events.append((q / CHAINS_A, lambda q=q: first(q)))
            for s in range(1, NY // 2):
                events.append((s + q / CHAINS_A, lambda q=q, s=s: all_a[q].step(s)))
            events.append((NY // 2 + q / CHAINS_A, lambda q=q: final(q)))
        for i in range(PARTS_A):
            last = (i + 1) * CHAINS_A // PARTS_A - 1
            events.append((NY // 2 + last / CHAINS_A + 0.01, lambda i=i: second(i)))
        run(events)
        finish(0, sum_a, z, a_in, in_a, 0, COLS_A)
        for m in [term_of_b(i) for i in range(nz)] + [m for chain in all_a for m in chain.sent()]:
            m.wait_send()

    def core_1():
        b_in = []

        def step(q, s):
            if q == 0:
                for i in (2 * s + 1, 2 * s + 2) if s else (0, 1, 2):
                    if i < nz:
                        term_of_b(i).wait_recv()
            all_b[q].step(s)

        def final(q):
            cols = slice(q * WIDE, (q + 1) * WIDE)
            for e, v in enumerate(all_b[q].final()):
                sum_b[:, e, :, cols] = v
                two_b[:, e, :, cols] = v.astype(BF16)

        def second(i):
            cols = slice(i * (wide - COLS_A) // PARTS_B, (i + 1) * (wide - COLS_A) // PARTS_B)
            b_in.extend(
                net.start(("b", i, d), two_b.at[lax.rem(y + d, NY), :, :, cols], in_b.at[d - 1, :, :, cols], along_y(d))
                for d in farthest_first(NY)
            )

        events = [(0.99, far_parts), (3.3, last_parts)]
        for q in range(chains_b):
            for s in range(half):
                events.append((s + q / chains_b, lambda q=q, s=s: step(q, s)))
            events.append((half + q / chains_b, lambda q=q: final(q)))
        for i in range(PARTS_B):
            last = (i + 1) * chains_b // PARTS_B - 1
            events.append((half + last / chains_b + 0.01, lambda i=i: second(i)))
        run(events)
        finish(1, sum_b, y, b_in, in_b, COLS_A, wide)
        for m in [term_of_a(q) for q in range(CHAINS_A)] + [m for chain in all_b for m in chain.sent()]:
            m.wait_send()

    pl.when(c == 0)(core_0)
    pl.when(c == 1)(core_1)
    for m in early:
        m.wait_send()


def pass_on(*refs):
    for i in range(4):
        refs[4 + i][...] = refs[i][...]


def solution(mesh):
    n_dp, n_ex = mesh.shape["dp"], mesh.shape["expert"]
    nz = n_dp // NY

    def body(tokens, cotangent, expert_ids, route_weights, expert_weights):
        count, width = tokens.shape
        slots = CAP * n_ex
        factor = 1.0 / math.sqrt(count * n_dp * n_ex)
        chains_a, chains_b = CHAINS_A, width // WIDE - CHAINS_A
        hr_a, hl_a = NY // 2, NY - 1 - NY // 2
        hr_b, hl_b = nz // 2, nz - 1 - nz // 2
        vmem = pl.BlockSpec(memory_space=pltpu.VMEM)
        count_messages = 7 + 6 + 6 + 2 + 8 + 6 + 7 + 2 + nz + chains_a + chains_a * (NY - 1) + chains_b * (nz - 1) + PARTS_A * (nz - 1) + PARTS_B * (NY - 1)
        lat, tg, rg, eg = pl.pallas_call(
            lambda *refs: kernel(nz, factor, *refs),
            out_shape=(
                jax.ShapeDtypeStruct((count, width), BF16),
                jax.ShapeDtypeStruct((count, width), BF16),
                jax.ShapeDtypeStruct((2, count), F32),
                jax.ShapeDtypeStruct((16, width), F32),
            ),
            in_specs=[pl.BlockSpec(memory_space=pltpu.HBM)] * 5,
            out_specs=(vmem,) * 4,
            scratch_shapes=[
                pltpu.VMEM((count, width), BF16),
                pltpu.VMEM((count, width), BF16),
                pltpu.VMEM((2, count), jnp.int32),
                pltpu.VMEM((2, count), BF16),
                pltpu.VMEM((3 * HID, width), BF16),
                pltpu.VMEM((7, count, width), BF16),
                pltpu.VMEM((7, count, width), BF16),
                pltpu.VMEM((8, 8, 128), F32),
                pltpu.VMEM((8, CAP, 128), BF16),
                pltpu.VMEM((2, slots, width), BF16),
                pltpu.VMEM((slots, width), BF16),
                pltpu.VMEM((slots, 3 * HID), BF16),
                pltpu.VMEM((8, count, width), BF16),
                pltpu.VMEM((8, count, width), BF16),
                pltpu.VMEM((4, count, width), BF16),
                pltpu.VMEM((4, count, width), BF16),
                pltpu.VMEM((4, count, width), BF16),
                pltpu.VMEM((4, count, width), BF16),
                pltpu.VMEM((6, count, width), BF16),
                pltpu.VMEM((8, 8, 128), F32),
                pltpu.VMEM((8, 8, 128), F32),
                pltpu.VMEM((nz, NY, 16, width), F32),
                pltpu.VMEM((nz, NY, 16, width), BF16),
                pltpu.VMEM((nz, NY, 16, width), BF16),
                pltpu.VMEM((16, width), F32),
                pltpu.VMEM((16, width), F32),
                pltpu.VMEM((chains_a, hr_a, 2, nz, 16, WIDE), BF16),
                pltpu.VMEM((chains_a, hr_a, 2, nz, 16, WIDE), BF16),
                pltpu.VMEM((chains_a, hl_a, 2, nz, 16, WIDE), BF16),
                pltpu.VMEM((chains_a, hl_a, 2, nz, 16, WIDE), BF16),
                pltpu.VMEM((chains_b, hr_b, 2, NY, 16, WIDE), BF16),
                pltpu.VMEM((chains_b, hr_b, 2, NY, 16, WIDE), BF16),
                pltpu.VMEM((chains_b, hl_b, 2, NY, 16, WIDE), BF16),
                pltpu.VMEM((chains_b, hl_b, 2, NY, 16, WIDE), BF16),
                pltpu.VMEM((nz, 2, 16, COLS_A), F32),
                pltpu.VMEM((NY, 2, 16, width - COLS_A), F32),
                pltpu.VMEM((nz, 2, 16, COLS_A), BF16),
                pltpu.VMEM((NY, 2, 16, width - COLS_A), BF16),
                pltpu.VMEM((nz - 1, 2, 16, COLS_A), BF16),
                pltpu.VMEM((NY - 1, 2, 16, width - COLS_A), BF16),
                pltpu.SemaphoreType.DMA((5,)),
                pltpu.SemaphoreType.DMA((count_messages,)),
                pltpu.SemaphoreType.DMA((count_messages,)),
            ],
            compiler_params=pltpu.CompilerParams(
                collective_id=0, has_side_effects=True, vmem_limit_bytes=62 * 1024 * 1024
            ),
        )(
            tokens,
            cotangent,
            expert_ids.T,
            route_weights.T,
            expert_weights.reshape(expert_weights.shape[1:]),
        )
        outs = (lat, tg, rg, eg)
        lat, tg, rg, eg = pl.pallas_call(
            pass_on,
            out_shape=tuple(jax.ShapeDtypeStruct(o.shape, o.dtype) for o in outs),
            in_specs=[vmem] * 4,
            out_specs=(vmem,) * 4,
            compiler_params=pltpu.CompilerParams(vmem_limit_bytes=62 * 1024 * 1024),
        )(*outs)
        return lat, tg, rg.T, eg[None]

    return jax.shard_map(
        body,
        mesh=mesh,
        in_specs=(
            P(("dp", "expert"), None),
            P(("dp", "expert"), None),
            P(("dp", "expert"), None),
            P(("dp", "expert"), None),
            P("expert", None, None),
        ),
        out_specs=(
            P(("dp", "expert"), None),
            P(("dp", "expert"), None),
            P(("dp", "expert"), None),
            P("expert", "dp", None),
        ),
        check_vma=False,
    )
```
